128 devices in a mesh: row: 8 (over y, core), col: 16 (over x, z).
Axes of the slice: x: 4, y: 4, z: 4, core: 2. Of those that a mesh axis runs over, the one named last changes fastest.
Arguments:
- atoms: bfloat16 [16384, 128], P(('row', 'col')), may hold values from -6 to 6
- atom_pair: bfloat16 [512, 16, 32, 128], P(('row', 'col')), may hold values from -6 to 6
- atom_token: int32 [16384], P(('row', 'col')), may hold values from 0 to 2047, as said below
- single: bfloat16 [2048, 768], P('row'), may hold values from -6 to 6
- pair: bfloat16 [2048, 2048, 128], P('row', 'col'), may hold values from -6 to 6
- atom_w: bfloat16 [128, 4, 128], replicated, may hold values from -0.5 to 0.5
- atom_pair_w: bfloat16 [16, 4], replicated, may hold values from -24 to 24
- atom_wo: bfloat16 [128, 128], replicated, may hold values from -0.5 to 0.5
- agg_w: bfloat16 [128, 768], replicated, may hold values from -0.5 to 0.5
- trans_in: bfloat16 [128, 2, 256], replicated, may hold values from -0.5 to 0.5
- trans_out: bfloat16 [256, 128], replicated, may hold values from -0.375 to 0.375
- bias_w: bfloat16 [128, 16], replicated, may hold values from -6 to 6
- token_w: bfloat16 [768, 4, 768], P(None, None, 'col'), may hold values from -0.21875 to 0.21875
- token_wo: bfloat16 [768, 768], P('col'), may hold values from -0.21875 to 0.21875
- back_w: bfloat16 [768, 128], P('col'), may hold values from -0.21875 to 0.21875
Outputs:
- single_out: bfloat16 [2048, 768], P('row', 'col')
- atoms_out: bfloat16 [16384, 128], P(('row', 'col'))
The draws below stay inside these ranges and needn't reach their ends.
Inputs may be any that keep to these rules, and one draw needn't show every extreme that they name: `atom_token`: atoms are in token order; the 2048 atoms of block b (b from 0) belong to tokens b * 256 to (b + 1) * 256 - 1; every token has 1 to 15 atoms, and in every block some token has exactly 15.
All inputs are finite; a program needn't handle non-finite values.
Results may differ from the reference program's by a relative error of at most 0.024.
The reference program's roundings to bfloat16 on the way count: a program that leaves them out, or rounds other values in their place, can miss the bound.
Values may be sent and summed in bfloat16 or wider, within the bound.
No kernel may reach another device: no remote copies, remote signals or barrier semaphores. Data moves between devices by JAX's collectives and lax.ppermute only.
A program may use at most 64 MiB of HBM per device.

```python
import math
import jax
import jax.numpy as jnp
from jax import lax

D = 768
HEADS = 16
HEAD = 48
CZ = 128
FFZ = 256
CA = 128
ATOM_HEADS = 4
ATOM_HEAD = 32
CP = 16
QW = 32
KW = 128
W_DEV = 4
TOKENS = 2048
TQ = 256
WINDOWS = 512
ATOMS = 16384
N_ROW = 8
N_COL = 16


def draw_atom_token(key, part):
    key = jax.random.fold_in(key, 5)
    per_row = QW * W_DEV * N_COL
    average = per_row // TQ
    half_rows = TQ // 2
    shift_key, order_key = jax.random.split(key)
    shifts = jax.random.randint(shift_key, (N_ROW, half_rows), 1 - average, average)
    shifts = shifts.at[:, 0].set(average - 1)
    counts = jnp.concatenate([average + shifts, average - shifts], axis=1)
    orders = jax.vmap(lambda row_key: jax.random.permutation(row_key, TQ))(jax.random.split(order_key, N_ROW))
    counts = jnp.take_along_axis(counts, orders, axis=1)
    bounds = jnp.cumsum(counts, axis=1)
    positions = jnp.arange(per_row)
    within = jnp.sum((bounds[:, None, :] <= positions[None, :, None]).astype(jnp.int32), axis=2)
    owners = within + (jnp.arange(N_ROW) * TQ)[:, None]
    return owners.reshape(ATOMS).astype(jnp.int32)


def draw_atom_pair_w(key, part):
    key = jax.random.fold_in(key, 11)
    values = jnp.clip(jax.random.normal(key, (CP, ATOM_HEADS), jnp.float32) * 0.5, -24.0, 24.0)
    return values.astype(jnp.bfloat16)


def draw_bias_w(key, part):
    key = jax.random.fold_in(key, 17)
    values = jnp.clip(jax.random.normal(key, (CZ, HEADS), jnp.float32) * (1.5 / CZ ** 0.5), -6.0, 6.0)
    return values.astype(jnp.bfloat16)


def levels(key, shape, cuts, least, top_value):
    def one(dim, blocks):
        heights = jax.random.uniform(jax.random.fold_in(jax.random.fold_in(key, 6), dim), (blocks,), jnp.float32, least / len(cuts), top_value / len(cuts))
        return jnp.repeat(jnp.exp(heights), shape[dim] // blocks).reshape((-1,) + (1,) * (len(shape) - dim - 1))

    gain = one(*cuts[0])
    for cut in cuts[1:]:
        gain = gain * one(*cut)
    return gain


def gaussian(own_key, shape, deviation, bound, pieces=(), held_as=jnp.bfloat16):
    array = jax.random.normal(own_key, shape, jnp.float32) * deviation
    if len(pieces) > 0:
        array = levels(own_key, shape, pieces, -0.22, 0.18) * array
    return jnp.clip(array, min=-bound, max=bound).astype(held_as)


def setup_inputs(seed: int = 0) -> dict:
    key_list = jax.random.split(jax.random.key(seed), 16)
    return {
        "atoms": gaussian(key_list[0], (ATOMS, CA), 1.0, 6.0, ((0, 128),)),
        "atom_pair": gaussian(key_list[1], (WINDOWS, CP, QW, KW), 1.0, 6.0, ((0, 128),)),
        "atom_token": draw_atom_token(jax.random.fold_in(key_list[15], 71), 0),
        "single": gaussian(key_list[3], (TOKENS, D), 1.0, 6.0, ((0, 8),)),
        "pair": gaussian(key_list[4], (TOKENS, TOKENS, CZ), 1.0, 6.0, ((0, 8), (1, 16))),
        "atom_w": gaussian(key_list[5], (CA, 4, CA), CA ** -0.5, 0.5),
        "atom_pair_w": draw_atom_pair_w(jax.random.fold_in(key_list[15], 71), 0),
        "atom_wo": gaussian(key_list[7], (CA, CA), CA ** -0.5, 0.5),
        "agg_w": gaussian(key_list[8], (CA, D), CA ** -0.5, 0.5),
        "trans_in": gaussian(key_list[9], (CZ, 2, FFZ), CZ ** -0.5, 0.5),
        "trans_out": gaussian(key_list[10], (FFZ, CZ), FFZ ** -0.5, 0.375),
        "bias_w": draw_bias_w(jax.random.fold_in(key_list[15], 71), 0),
        "token_w": gaussian(key_list[12], (D, 4, D), D ** -0.5, 0.21875, ((2, 16),)),
        "token_wo": gaussian(key_list[13], (D, D), D ** -0.5, 0.21875, ((0, 16),)),
        "back_w": gaussian(key_list[14], (D, CA), D ** -0.5, 0.21875, ((0, 16),)),
    }


epsilon = 1e-05
masked_score = -1e+30

def layer_norm(values):
    centred = values - lax.optimization_barrier(jnp.mean(values, axis=-1, keepdims=True))
    spread = lax.optimization_barrier(jnp.mean(centred * centred, axis=-1, keepdims=True))
    return centred * lax.rsqrt(spread + epsilon)

def rounded(values):
    return lax.optimization_barrier(values.astype(jnp.bfloat16))

def softmax_rows(scores):
    highest = lax.optimization_barrier(jnp.max(scores, axis=-1, keepdims=True))
    raised = jnp.exp(scores - highest)
    return (raised / lax.optimization_barrier(jnp.sum(raised, axis=-1, keepdims=True))).astype(jnp.bfloat16)

def pair_block(tile, trans_in, trans_out, bias_w):
    normed = layer_norm(tile.astype(jnp.float32)).astype(jnp.bfloat16)
    both = jnp.einsum('ijc,cmf->ijmf', normed.astype(jnp.float32), trans_in.astype(jnp.float32))
    hidden = (jax.nn.silu(both[:, :, 0, :]) * both[:, :, 1, :]).astype(jnp.bfloat16)
    update = jnp.einsum('ijf,fc->ijc', hidden.astype(jnp.float32), trans_out.astype(jnp.float32))
    renewed = rounded(tile.astype(jnp.float32) + update)
    renormed = layer_norm(renewed.astype(jnp.float32)).astype(jnp.bfloat16)
    return jnp.einsum('ijc,ch->hij', renormed.astype(jnp.float32), bias_w.astype(jnp.float32)).astype(jnp.bfloat16)

def split_heads(block):
    return block.reshape(TOKENS, HEADS, HEAD).transpose(1, 0, 2)

def one_head(operands):
    query_head, key_head, value_head, bias_head = operands
    scores = jnp.dot(query_head, key_head.T, preferred_element_type=jnp.float32) / math.sqrt(HEAD)
    weights = softmax_rows(scores + bias_head.astype(jnp.float32))
    return jnp.dot(weights, value_head, preferred_element_type=jnp.float32)

def reference(atoms, atom_pair, atom_token, single, pair, atom_w, atom_pair_w, atom_wo, agg_w, trans_in, trans_out, bias_w, token_w, token_wo, back_w):
    rim = (KW - QW) // 2
    atom_norm = layer_norm(atoms.astype(jnp.float32)).astype(jnp.bfloat16)
    projected = jnp.einsum('ac,cmd->amd', atom_norm.astype(jnp.float32), atom_w.astype(jnp.float32)).astype(jnp.bfloat16)
    padded = jnp.pad(projected, ((rim, rim), (0, 0), (0, 0)))
    key_index = (jnp.arange(WINDOWS) * QW)[:, None] + jnp.arange(KW)[None, :]
    window_keys = padded[key_index]
    inside = (key_index >= rim) & (key_index < ATOMS + rim)
    queries = projected[:, 0, :].astype(jnp.float32).reshape(WINDOWS, QW, ATOM_HEADS, ATOM_HEAD)
    key_part = window_keys[:, :, 1, :].astype(jnp.float32).reshape(WINDOWS, KW, ATOM_HEADS, ATOM_HEAD)
    value_part = window_keys[:, :, 2, :].astype(jnp.float32).reshape(WINDOWS, KW, ATOM_HEADS, ATOM_HEAD)
    atom_bias = jnp.einsum('wcij,ch->whij', atom_pair.astype(jnp.float32), atom_pair_w.astype(jnp.float32))
    scores = jnp.einsum('wiha,wjha->whij', queries, key_part) / math.sqrt(ATOM_HEAD) + atom_bias
    scores = jnp.where(inside[:, None, None, :], scores, masked_score)
    weights = softmax_rows(scores)
    attended = jnp.einsum('whij,wjha->wiha', weights.astype(jnp.float32), value_part).reshape(ATOMS, CA)
    gated = (jax.nn.sigmoid(projected[:, 3, :].astype(jnp.float32)) * attended).astype(jnp.bfloat16)
    atoms_mid = rounded(atoms.astype(jnp.float32) + jnp.dot(gated, atom_wo, preferred_element_type=jnp.float32))
    features = jax.nn.relu(jnp.dot(atoms_mid, agg_w, preferred_element_type=jnp.float32)).astype(jnp.bfloat16)
    token_sum = jax.ops.segment_sum(features.astype(jnp.float32), atom_token, num_segments=TOKENS)
    token_count = jax.ops.segment_sum(jnp.ones((ATOMS,), jnp.float32), atom_token, num_segments=TOKENS)
    token_in = rounded(single.astype(jnp.float32) + token_sum / token_count[:, None])
    blocks = pair.reshape(TOKENS // 32, 32, TOKENS, CZ)
    bias_blocks = lax.map(lambda tile: pair_block(tile, trans_in, trans_out, bias_w), blocks)
    pair_bias = jnp.moveaxis(bias_blocks, 1, 0).reshape(HEADS, TOKENS, TOKENS)
    token_norm = layer_norm(token_in.astype(jnp.float32)).astype(jnp.bfloat16)
    token_proj = jnp.einsum('td,dme->tme', token_norm.astype(jnp.float32), token_w.astype(jnp.float32)).astype(jnp.bfloat16)
    heads_out = lax.map(one_head, (split_heads(token_proj[:, 0, :]), split_heads(token_proj[:, 1, :]), split_heads(token_proj[:, 2, :]), pair_bias))
    token_attn = heads_out.transpose(1, 0, 2).reshape(TOKENS, D)
    token_gated = (jax.nn.sigmoid(token_proj[:, 3, :].astype(jnp.float32)) * token_attn).astype(jnp.bfloat16)
    single_out = (token_in.astype(jnp.float32) + jnp.dot(token_gated, token_wo, preferred_element_type=jnp.float32)).astype(jnp.bfloat16)
    atom_back = jnp.dot(single_out, back_w, preferred_element_type=jnp.float32).astype(jnp.bfloat16)
    atoms_out = (atoms_mid.astype(jnp.float32) + atom_back[atom_token].astype(jnp.float32)).astype(jnp.bfloat16)
    return (single_out, atoms_out)
```

```python
import functools
import math

import jax
import jax.numpy as jnp
from jax import lax
from jax.experimental import pallas as pl
from jax.experimental.pallas import tpu as pltpu
from jax.sharding import PartitionSpec as P

HEADS = 16
HEAD = 48
CA = 128
CZ = 128
ATOM_HEADS = 4
ATOM_HEAD = 32
QW = 32
KW = 128
RIM = (KW - QW) // 2
PAIR_ROWS = 32
FIRST_ROWS = 64
MIB = 2**20

epsilon = 1e-05
masked_score = -1e30
bf16 = jnp.bfloat16
f32 = jnp.float32


def dot(a, b):
    return jnp.dot(a, b, preferred_element_type=f32)


def dot_t(a, b):
    return lax.dot_general(a, b, (((1,), (1,)), ((), ())), preferred_element_type=f32)


def layer_norm(values):
    centred = values - jnp.mean(values, axis=-1, keepdims=True)
    spread = jnp.mean(centred * centred, axis=-1, keepdims=True)
    return centred * lax.rsqrt(spread + epsilon)


def whole(array):
    return pl.BlockSpec(array.shape, lambda *_: (0,) * array.ndim)


def params(mib=48):
    return pltpu.CompilerParams(vmem_limit_bytes=mib * MIB)


def cost(flops, moved):
    return pl.CostEstimate(flops=flops, bytes_accessed=moved, transcendentals=0)


def atom_kernel(
    place_ref, pair_w_ref, before_ref, own_ref, after_ref, atom_pair_ref, token_ref, w_ref, wo_ref,
    mid_ref, send_ref,
):
    device, row, last = place_ref[0], place_ref[1], place_ref[2]
    atoms = own_ref[...].astype(f32)
    count = atoms.shape[0]
    extended = jnp.concatenate([before_ref[...].astype(f32), atoms, after_ref[...].astype(f32)], axis=0)
    norm = layer_norm(extended).astype(bf16)
    projected = dot(norm, w_ref[...]).astype(bf16)
    lanes = lax.broadcasted_iota(jnp.int32, (1, CA), 1) // ATOM_HEAD
    keys = lax.broadcasted_iota(jnp.int32, (1, KW), 1)
    parts = []
    for window in range(count // QW):
        start = window * QW
        query = projected[RIM + start : RIM + start + QW, :CA]
        query = jnp.concatenate(
            [jnp.where(lanes == head, query, jnp.zeros_like(query)) for head in range(ATOM_HEADS)], axis=0
        )
        key = projected[start : start + KW, CA : 2 * CA]
        value = projected[start : start + KW, 2 * CA : 3 * CA]
        planes = [atom_pair_ref[window, c].astype(f32) for c in range(atom_pair_ref.shape[1])]
        bias = []
        for head in range(ATOM_HEADS):
            total = planes[0] * pair_w_ref[0, head]
            for c in range(1, len(planes)):
                total = total + planes[c] * pair_w_ref[c, head]
            bias.append(total)
        scores = dot_t(query, key) / math.sqrt(ATOM_HEAD) + jnp.concatenate(bias, axis=0)
        position = device * count - RIM + start + keys
        scores = jnp.where((position >= 0) & (position < last), scores, masked_score)
        raised = jnp.exp(scores - jnp.max(scores, axis=-1, keepdims=True))
        weights = (raised / jnp.sum(raised, axis=-1, keepdims=True)).astype(bf16)
        mixed = dot(weights, value)
        out = jnp.zeros((QW, CA), f32)
        for head in range(ATOM_HEADS):
            out = out + jnp.where(lanes == head, mixed[head * QW : (head + 1) * QW], 0.0)
        parts.append(out)
    attended = jnp.concatenate(parts, axis=0)
    gate = projected[RIM : RIM + count, 3 * CA :].astype(f32)
    gated = (jax.nn.sigmoid(gate) * attended).astype(bf16)
    mid = (atoms + dot(gated, wo_ref[...])).astype(bf16)
    mid_ref[...] = mid
    local = (token_ref[...] - row).astype(f32).astype(bf16)
    tail = jnp.broadcast_to(local, (16, count))
    for target in range(send_ref.shape[0]):
        send_ref[target, :count, :] = mid
        send_ref[target, count:, :] = tail


def pair_body(pair_ref, centre_ref, win_ref, wout_ref, wb_ref, out_ref, hold_ref):
    rows = pair_ref.shape[0]
    tile = pair_ref[...].reshape(rows * pair_ref.shape[1], CZ)
    centred = dot_t(centre_ref[...], tile)
    spread = jnp.sum(centred * centred, axis=0, keepdims=True) * (1.0 / CZ)
    normed = (centred * lax.rsqrt(spread + epsilon)).astype(bf16)
    both = dot(win_ref[...], normed)
    half = both.shape[0] // 2
    gate, up = both[:half], both[half:]
    hidden = ((gate * jnp.tanh(gate) + gate) * up).astype(bf16)
    renewed = centred + dot(wout_ref[...], hidden)
    spread = jnp.sum(renewed * renewed, axis=0, keepdims=True) * (1.0 / CZ)
    bias = dot(wb_ref[...], renewed.astype(bf16)) * lax.rsqrt(spread + epsilon)
    width = pair_ref.shape[1]
    for i in range(rows):
        hold_ref[:, i, :] = bias[:, i * width : (i + 1) * width]
    out_ref[...] = hold_ref[...].astype(bf16)


def pair_first(*refs):
    pair_body(*refs)


def pair_rest(_, *refs):
    pair_body(*refs)


def pair_call(pair, weights, start, stop, partial_out):
    steps = (stop - start) // PAIR_ROWS
    skip = start // PAIR_ROWS
    rows, cols, _ = pair.shape
    in_specs = [pl.BlockSpec((PAIR_ROWS, cols, CZ), lambda i: (i + skip, 0, 0))] + [whole(w) for w in weights]
    operands = (pair, *weights)
    aliases = {}
    kernel = pair_first
    if partial_out is not None:
        in_specs = [pl.BlockSpec(memory_space=pl.ANY)] + in_specs
        operands = (partial_out, *operands)
        aliases = {0: 0}
        kernel = pair_rest
    positions = (stop - start) * cols
    return pl.pallas_call(
        kernel,
        grid=(steps,),
        in_specs=in_specs,
        out_specs=pl.BlockSpec((HEADS, PAIR_ROWS, cols), lambda i: (0, i + skip, 0)),
        out_shape=jax.ShapeDtypeStruct((HEADS, rows, cols), bf16),
        scratch_shapes=[pltpu.VMEM((HEADS, PAIR_ROWS, cols), f32)],
        input_output_aliases=aliases,
        compiler_params=params(56),
        cost_estimate=cost(positions * 620_000, positions * 288),
        name="pair_bias",
    )(*operands)


def token_kernel(got_ref, single_ref, agg_ref, wq_ref, wt_ref, in_ref, query_ref, gate_ref, send_ref):
    sources, count = got_ref.shape[0], got_ref.shape[2]
    tokens = single_ref.shape[0]
    mids = jnp.concatenate([got_ref[s, :count, :] for s in range(sources)], axis=0)
    features = jnp.maximum(dot(mids, agg_ref[...]), 0.0).astype(bf16)
    token = lax.broadcasted_iota(jnp.int32, (tokens, count), 0).astype(f32)
    onehot = jnp.concatenate(
        [
            jnp.where(token == got_ref[s, count : count + 16, :].astype(f32)[:1], 1.0, 0.0)
            for s in range(sources)
        ],
        axis=1,
    )
    token_count = jnp.sum(onehot, axis=1, keepdims=True)
    token_sum = dot(onehot.astype(bf16), features)
    token_in = (single_ref[...].astype(f32) + token_sum / token_count).astype(bf16)
    in_ref[...] = token_in
    norm = layer_norm(token_in.astype(f32)).astype(bf16)
    query_ref[...] = dot(norm, wq_ref[...]).astype(bf16)
    rest = dot_t(wt_ref[...], norm).astype(bf16)
    gate_ref[...] = rest[2 * HEAD :]
    for target in range(send_ref.shape[0]):
        send_ref[target] = rest[: 2 * HEAD]


def attention_kernel(query_ref, gate_ref, kv_ref, bias_ref, send_ref):
    rows = kv_ref.shape[0]
    per = bias_ref.shape[0] // rows
    scores = jnp.concatenate(
        [
            dot(query_ref[...], kv_ref[r, :HEAD, :]) / math.sqrt(HEAD)
            + jnp.concatenate([bias_ref[r * per + k].astype(f32) for k in range(per)], axis=1)
            for r in range(rows)
        ],
        axis=1,
    )
    raised = jnp.exp(scores - jnp.max(scores, axis=-1, keepdims=True))
    weights = (raised / jnp.sum(raised, axis=-1, keepdims=True)).astype(bf16)
    values = jnp.concatenate([kv_ref[r, HEAD:, :] for r in range(rows)], axis=1)
    attended = dot_t(values, weights)
    gated = (jax.nn.sigmoid(gate_ref[...].astype(f32)) * attended).astype(bf16)
    for target in range(send_ref.shape[0]):
        send_ref[target] = gated


def final_kernel(place_ref, got_ref, in_ref, weights_ref, mid_ref, token_ref, single_ref, atoms_ref):
    heads, head, tokens = got_ref.shape
    width = in_ref.shape[1]
    gated = got_ref[...].reshape(heads * head, tokens).T
    single = (in_ref[...].astype(f32) + dot(gated, weights_ref[:, :width])).astype(bf16)
    mine = single_ref.shape[1]
    column = lax.broadcasted_iota(jnp.int32, (width, mine), 0)
    wanted = lax.broadcasted_iota(jnp.int32, (width, mine), 1) + place_ref[3] * mine
    select = jnp.where(column == wanted, 1.0, 0.0).astype(bf16)
    single_ref[...] = dot(single, select).astype(bf16)
    back = dot(single, weights_ref[:, width:]).astype(bf16)
    count = mid_ref.shape[0]
    token = lax.broadcasted_iota(jnp.int32, (tokens, count), 0)
    onehot = jnp.where(token == token_ref[...] - place_ref[1], 1.0, 0.0)
    picked = dot(onehot.T.astype(bf16), back)
    atoms_ref[...] = (mid_ref[...].astype(f32) + picked).astype(bf16)


def body(
    atoms,
    atom_pair,
    atom_token,
    single,
    pair,
    atom_w,
    atom_pair_w,
    atom_wo,
    agg_w,
    trans_in,
    trans_out,
    bias_w,
    token_w,
    token_wo,
    back_w,
):
    row_size, col_size = lax.axis_size("row"), lax.axis_size("col")
    count = atoms.shape[0]
    query_rows, width = single.shape
    both = ("row", "col")
    devices = row_size * col_size
    up = [(i, i + 1) for i in range(devices - 1)]
    down = [(j, i) for i, j in up]
    before = lax.ppermute(atoms[count - RIM :], both, up)
    after = lax.ppermute(atoms[:RIM], both, down)
    out_weights = lax.all_gather(jnp.concatenate([token_wo, back_w], axis=1), "col", axis=0, tiled=True)

    device = lax.axis_index(both)
    place = jnp.stack(
        [
            device,
            lax.axis_index("row") * query_rows,
            jnp.asarray(count * devices, device.dtype),
            lax.axis_index("col"),
        ]
    ).astype(jnp.int32)
    smem = pl.BlockSpec(memory_space=pltpu.SMEM)
    token_row = atom_token.reshape(1, count)

    centre = (jnp.eye(CZ, dtype=f32) - 1.0 / CZ).astype(bf16)
    half = jnp.asarray(0.5, bf16)
    win = jnp.concatenate([trans_in[:, 0, :] * half, trans_in[:, 1, :]], axis=1).T
    wout = dot_t(centre, trans_out).astype(bf16)
    pair_weights = (centre, win, wout, bias_w.T)
    bias = pair_call(pair, pair_weights, 0, FIRST_ROWS, None)

    atom_weights = atom_w.reshape(CA, 4 * CA)
    vmem = pl.BlockSpec(memory_space=pltpu.VMEM)
    mid, mid_send = pl.pallas_call(
        atom_kernel,
        in_specs=[smem, smem] + [vmem] * 7,
        out_specs=[vmem, vmem],
        out_shape=[
            jax.ShapeDtypeStruct((count, CA), bf16),
            jax.ShapeDtypeStruct((col_size, count + 16, CA), bf16),
        ],
        compiler_params=params(),
        cost_estimate=cost(4_000_000_000, 2_000_000),
        name="atom_stage",
    )(place, atom_pair_w.astype(f32), before, atoms, after, atom_pair, token_row, atom_weights, atom_wo)
    mids = lax.all_to_all(mid_send, "col", split_axis=0, concat_axis=0, tiled=True)

    bias = pair_call(pair, pair_weights, FIRST_ROWS, query_rows, bias)
    bias_rows = lax.all_to_all(bias, "col", split_axis=0, concat_axis=0, tiled=True)

    turned = jnp.transpose(token_w[:, 1:, :], (1, 2, 0)).reshape(3 * HEAD, width)
    token_in, query, gate, kv_send = pl.pallas_call(
        token_kernel,
        in_specs=[vmem] * 5,
        out_specs=[vmem] * 4,
        out_shape=[
            jax.ShapeDtypeStruct((query_rows, width), bf16),
            jax.ShapeDtypeStruct((query_rows, HEAD), bf16),
            jax.ShapeDtypeStruct((HEAD, query_rows), bf16),
            jax.ShapeDtypeStruct((row_size, 2 * HEAD, query_rows), bf16),
        ],
        compiler_params=params(),
        cost_estimate=cost(4_000_000_000, 2_000_000),
        name="token_stage",
    )(mids, single, agg_w, token_w[:, 0, :], turned)
    kv = lax.all_to_all(kv_send, "row", split_axis=0, concat_axis=0, tiled=True)

    gated_send = pl.pallas_call(
        attention_kernel,
        in_specs=[vmem] * 4,
        out_specs=vmem,
        out_shape=jax.ShapeDtypeStruct((col_size, HEAD, query_rows), bf16),
        compiler_params=params(),
        cost_estimate=cost(3_000_000_000, 2_000_000),
        name="token_attention",
    )(query, gate, kv, bias_rows)
    gated = lax.all_to_all(gated_send, "col", split_axis=0, concat_axis=0, tiled=True)

    return pl.pallas_call(
        final_kernel,
        in_specs=[smem] + [vmem] * 5,
        out_specs=[vmem, vmem],
        out_shape=[
            jax.ShapeDtypeStruct((query_rows, width // col_size), bf16),
            jax.ShapeDtypeStruct((count, CA), bf16),
        ],
        compiler_params=params(),
        cost_estimate=cost(3_000_000_000, 2_000_000),
        name="token_out",
    )(place, gated, token_in, out_weights, mid, token_row)


def solution(mesh):
    in_specs = (
        P(("row", "col"), None),
        P(("row", "col"), None, None, None),
        P(("row", "col")),
        P("row", None),
        P("row", "col", None),
        P(),
        P(),
        P(),
        P(),
        P(),
        P(),
        P(),
        P(None, None, "col"),
        P("col", None),
        P("col", None),
    )
    out_specs = (P("row", "col"), P(("row", "col"), None))
    return jax.shard_map(body, mesh=mesh, in_specs=in_specs, out_specs=out_specs, check_vma=False)
```

```python
import functools
import math

import jax
import jax.numpy as jnp
from jax import lax
from jax.experimental import pallas as pl
from jax.experimental.pallas import tpu as pltpu
from jax.sharding import PartitionSpec as P

HEADS = 16
HEAD = 48
CA = 128
CZ = 128
ATOM_HEADS = 4
ATOM_HEAD = 32
QW = 32
KW = 128
RIM = (KW - QW) // 2
PAIR_ROWS = 32
FIRST_ROWS = 64
MIB = 2**20
DONE = jax.ShapeDtypeStruct((8, 128), jnp.float32)

epsilon = 1e-05
masked_score = -1e30
bf16 = jnp.bfloat16
f32 = jnp.float32


def dot(a, b):
    return jnp.dot(a, b, preferred_element_type=f32)


def dot_t(a, b):
    return lax.dot_general(a, b, (((1,), (1,)), ((), ())), preferred_element_type=f32)


def layer_norm(values):
    centred = values - jnp.mean(values, axis=-1, keepdims=True)
    spread = jnp.mean(centred * centred, axis=-1, keepdims=True)
    return centred * lax.rsqrt(spread + epsilon)


def params(mib=24):
    return pltpu.CompilerParams(vmem_limit_bytes=mib * MIB)


def cost(flops, moved):
    return pl.CostEstimate(flops=flops, bytes_accessed=moved, transcendentals=0)


def atom_kernel(
    _, place_ref, before_ref, own_ref, after_ref, atom_pair_ref, pair_w_ref, token_ref, w_ref, wo_ref, out_w_ref,
    back_w_ref, mid_ref, send_ref, done_ref,
):
    done_ref[...] = jnp.zeros_like(done_ref)
    device, row, last = place_ref[0], place_ref[1], place_ref[2]
    atoms = own_ref[...].astype(f32)
    count = atoms.shape[0]
    extended = jnp.concatenate(
        [before_ref[count - RIM :, :].astype(f32), atoms, after_ref[:RIM, :].astype(f32)], axis=0
    )
    norm = layer_norm(extended).astype(bf16)
    wide = w_ref[...].astype(f32)
    query_all, key_all, value_all, gate_all = [dot(norm, wide[:, m, :].astype(bf16)).astype(bf16) for m in range(4)]
    lanes = lax.broadcasted_iota(jnp.int32, (1, CA), 1) // ATOM_HEAD
    keys = lax.broadcasted_iota(jnp.int32, (1, KW), 1)
    mix = pair_w_ref[...].astype(f32)
    parts = []
    for window in range(count // QW):
        start = window * QW
        query = query_all[RIM + start : RIM + start + QW]
        query = jnp.concatenate(
            [jnp.where(lanes == head, query, jnp.zeros_like(query)) for head in range(ATOM_HEADS)], axis=0
        )
        key = key_all[start : start + KW]
        value = value_all[start : start + KW]
        planes = [atom_pair_ref[window, c].astype(f32) for c in range(atom_pair_ref.shape[1])]
        bias = []
        for head in range(ATOM_HEADS):
            total = planes[0] * mix[head : head + 1, 0:1]
            for c in range(1, len(planes)):
                total = total + planes[c] * mix[head : head + 1, c : c + 1]
            bias.append(total)
        scores = dot_t(query, key) / math.sqrt(ATOM_HEAD) + jnp.concatenate(bias, axis=0)
        position = device * count - RIM + start + keys
        scores = jnp.where((position >= 0) & (position < last), scores, masked_score)
        raised = jnp.exp(scores - jnp.max(scores, axis=-1, keepdims=True))
        weights = (raised / jnp.sum(raised, axis=-1, keepdims=True)).astype(bf16)
        mixed = dot(weights, value)
        out = jnp.zeros((QW, CA), f32)
        for head in range(ATOM_HEADS):
            out = out + jnp.where(lanes == head, mixed[head * QW : (head + 1) * QW], 0.0)
        parts.append(out)
    attended = jnp.concatenate(parts, axis=0)
    gate = gate_all[RIM : RIM + count].astype(f32)
    gated = (jax.nn.sigmoid(gate) * attended).astype(bf16)
    mid = (atoms + dot(gated, wo_ref[...])).astype(bf16)
    mid_ref[...] = mid
    local = (token_ref[...] - row).astype(f32).astype(bf16)
    tail = jnp.broadcast_to(local, (16, count))
    back_w = back_w_ref[...]
    rows, width = out_w_ref.shape
    targets = send_ref.shape[0]
    mine = width // targets
    out_w = out_w_ref[...].astype(f32)
    blank = jnp.zeros((rows, CA - mine), bf16)
    for target in range(targets):
        send_ref[target, :count, :] = mid
        send_ref[target, count : count + 16, :] = tail
        send_ref[target, count + 16 : count + 16 + rows, :] = back_w
        part = out_w[:, target * mine : (target + 1) * mine].astype(bf16)
        send_ref[target, count + 16 + rows :, :] = jnp.concatenate([part, blank], axis=1)


def pair_body(pair_ref, win_ref, wout_ref, wb_ref, out_ref, hold_ref):
    rows = pair_ref.shape[0]
    tile = pair_ref[...].reshape(rows * pair_ref.shape[1], CZ)
    centred = dot_t(centre(), tile)
    spread = jnp.sum(centred * centred, axis=0, keepdims=True) * (1.0 / CZ)
    normed = (centred * lax.rsqrt(spread + epsilon)).astype(bf16)
    both = dot(win_ref[...], normed)
    half = both.shape[0] // 2
    gate, up = both[:half], both[half:]
    hidden = ((gate * jnp.tanh(gate) + gate) * up).astype(bf16)
    renewed = centred + dot(wout_ref[...], hidden)
    spread = jnp.sum(renewed * renewed, axis=0, keepdims=True) * (1.0 / CZ)
    bias = dot(wb_ref[...], renewed.astype(bf16)) * lax.rsqrt(spread + epsilon)
    width = pair_ref.shape[1]
    for i in range(rows):
        hold_ref[:, i, :] = bias[:, i * width : (i + 1) * width]
    out_ref[...] = hold_ref[...].astype(bf16)


def centre():
    row = lax.broadcasted_iota(jnp.int32, (CZ, CZ), 0)
    column = lax.broadcasted_iota(jnp.int32, (CZ, CZ), 1)
    return (jnp.where(row == column, 1.0, 0.0) - 1.0 / CZ).astype(bf16)


def pair_first(pair_ref, trans_in_ref, trans_out_ref, wb_ref, out_ref, done_ref, win_ref, wout_ref, hold_ref):
    @pl.when(pl.program_id(0) == 0)
    def _():
        wide = trans_in_ref[...].astype(f32)
        units = wide.shape[2]
        win_ref[:units, :] = (wide[:, 0, :].T * 0.5).astype(bf16)
        win_ref[units:, :] = wide[:, 1, :].T.astype(bf16)
        wout_ref[...] = dot_t(centre(), trans_out_ref[...]).astype(bf16)

    pair_body(pair_ref, win_ref, wout_ref, wb_ref, out_ref, hold_ref)
    done_ref[...] = jnp.zeros_like(done_ref)


def pair_rest(_, __, pair_ref, win_ref, wout_ref, wb_ref, out_ref, done_ref, hold_ref):
    pair_body(pair_ref, win_ref, wout_ref, wb_ref, out_ref, hold_ref)
    done_ref[...] = jnp.zeros_like(done_ref)


def pair_call(kernel, pair, weights, start, stop, before, out_weights):
    steps = (stop - start) // PAIR_ROWS
    vmem = pl.BlockSpec(memory_space=pltpu.VMEM)
    skip = start // PAIR_ROWS
    rows, cols, _ = pair.shape
    in_specs = [pl.BlockSpec(memory_space=pl.ANY), vmem] if before else []
    in_specs += [pl.BlockSpec((PAIR_ROWS, cols, CZ), lambda i: (i + skip, 0, 0))] + [vmem] * len(weights)
    positions = (stop - start) * cols
    return pl.pallas_call(
        kernel,
        grid=(steps,),
        in_specs=in_specs,
        out_specs=[pl.BlockSpec((HEADS, PAIR_ROWS, cols), lambda i: (0, i + skip, 0))]
        + [vmem] * (1 + len(out_weights)),
        out_shape=[jax.ShapeDtypeStruct((HEADS, rows, cols), bf16), DONE, *out_weights],
        scratch_shapes=[pltpu.VMEM((HEADS, PAIR_ROWS, cols), f32)],
        input_output_aliases={0: 0} if before else {},
        compiler_params=params(56),
        cost_estimate=cost(positions * 620_000, positions * 288),
        name="pair_bias",
    )(*before, pair, *weights)


def token_kernel(
    _, got_ref, single_ref, agg_ref, w_ref, out_w_ref, in_ref, held_ref, send_ref
):
    sources, count = got_ref.shape[0], got_ref.shape[2]
    tokens = single_ref.shape[0]
    mids = jnp.concatenate([got_ref[s, :count, :] for s in range(sources)], axis=0)
    features = jnp.maximum(dot(mids, agg_ref[...]), 0.0).astype(bf16)
    token = lax.broadcasted_iota(jnp.int32, (tokens, count), 0).astype(f32)
    onehot = jnp.concatenate(
        [
            jnp.where(token == got_ref[s, count : count + 16, :].astype(f32)[:1], 1.0, 0.0)
            for s in range(sources)
        ],
        axis=1,
    )
    token_count = jnp.sum(onehot, axis=1, keepdims=True)
    token_sum = dot(onehot.astype(bf16), features)
    token_in = (single_ref[...].astype(f32) + token_sum / token_count).astype(bf16)
    in_ref[...] = token_in
    norm = layer_norm(token_in.astype(f32)).astype(bf16)
    turned = dot_t(w_ref[...], norm).astype(bf16)
    held_ref[:, :tokens] = turned[:HEAD]
    held_ref[:, tokens : 2 * tokens] = turned[3 * HEAD :]
    send_ref[...] = turned[HEAD : 3 * HEAD]
    rows = out_w_ref.shape[0]
    back_w = jnp.concatenate(
        [got_ref[s, count + 16 : count + 16 + rows, :] for s in range(sources)], axis=0
    )
    held_ref[:, 2 * tokens :] = dot(out_w_ref[...], back_w).astype(bf16)


def attention_kernel(place_ref, held_ref, bias_ref, *refs):
    *kv_refs, send_ref, done_ref = refs
    done_ref[...] = jnp.zeros_like(done_ref)
    rows = len(kv_refs)
    tokens = kv_refs[0].shape[1]
    query = held_ref[:, :tokens].astype(f32).T.astype(bf16)
    per = bias_ref.shape[0] // rows
    scores = []
    for step, kv_ref in enumerate(kv_refs):
        source = lax.rem(place_ref[4] + rows - step, rows) * per
        bias = jnp.concatenate([bias_ref[source + k].astype(f32) for k in range(per)], axis=1)
        scores.append(dot(query, kv_ref[:HEAD, :]) / math.sqrt(HEAD) + bias)
    scores = jnp.concatenate(scores, axis=1)
    raised = jnp.exp(scores - jnp.max(scores, axis=-1, keepdims=True))
    weights = (raised / jnp.sum(raised, axis=-1, keepdims=True)).astype(bf16)
    values = jnp.concatenate([kv_ref[HEAD:, :] for kv_ref in kv_refs], axis=1)
    attended = dot_t(values, weights)
    gate = held_ref[:, tokens : 2 * tokens].astype(f32)
    gated = (jax.nn.sigmoid(gate) * attended).astype(bf16)
    back = held_ref[:, 2 * tokens :]
    for target in range(send_ref.shape[0]):
        send_ref[target, :, :tokens] = gated
        send_ref[target, :, tokens:] = back


def ready_kernel(_, place_ref, got_ref, in_ref, token_ref, out_w_ref, own_ref, back_ref, onehot_ref):
    sources, count = got_ref.shape[0], got_ref.shape[2]
    tokens, width = in_ref.shape
    mine = width // sources
    token_in = in_ref[...]
    start = count + 16
    back_w = jnp.concatenate([got_ref[s, start : start + mine, :] for s in range(sources)], axis=0)
    out_w = jnp.concatenate([got_ref[s, start + mine :, :] for s in range(sources)], axis=0)
    out_w_ref[...] = out_w.astype(f32).T[:mine].astype(bf16)
    back_ref[...] = dot_t(back_w.astype(f32).T.astype(bf16), token_in)
    wanted = lax.broadcasted_iota(jnp.int32, (mine, width), 0) + place_ref[3] * mine
    column = lax.broadcasted_iota(jnp.int32, (mine, width), 1)
    own_ref[...] = dot_t(jnp.where(column == wanted, 1.0, 0.0).astype(bf16), token_in)
    token = lax.broadcasted_iota(jnp.int32, (tokens, count), 0)
    onehot = jnp.where(token == token_ref[...] - place_ref[1], 1.0, 0.0)
    onehot_ref[...] = onehot.T.astype(bf16)


def final_kernel(got_ref, out_w_ref, own_ref, back_ref, onehot_ref, mid_ref, single_ref, atoms_ref):
    heads, head, _ = got_ref.shape
    tokens = own_ref.shape[1]
    gated = got_ref[:, :, :tokens].reshape(heads * head, tokens)
    mixed = got_ref[:, :, tokens:].reshape(heads * head, CA)
    single_ref[...] = (own_ref[...] + dot(out_w_ref[...], gated)).astype(bf16)
    back = (back_ref[...] + dot(mixed.astype(f32).T.astype(bf16), gated)).astype(bf16)
    picked = dot_t(onehot_ref[...], back)
    atoms_ref[...] = (mid_ref[...].astype(f32) + picked).astype(bf16)


def shape(*sizes, dtype=bf16):
    return jax.ShapeDtypeStruct(sizes, dtype)


def single_step(kernel, name, in_specs, out_shape, flops, moved, operands):
    return pl.pallas_call(
        kernel,
        in_specs=in_specs,
        out_specs=[pl.BlockSpec(memory_space=pltpu.VMEM)] * len(out_shape),
        out_shape=out_shape,
        compiler_params=params(),
        cost_estimate=cost(flops, moved),
        name=name,
    )(*operands)


def gathered(copies, axis):
    return lax.all_to_all(copies, axis, split_axis=0, concat_axis=0, tiled=True)


def body(
    atoms,
    atom_pair,
    atom_token,
    single,
    pair,
    atom_w,
    atom_pair_w,
    atom_wo,
    agg_w,
    trans_in,
    trans_out,
    bias_w,
    token_w,
    token_wo,
    back_w,
):
    row_size, col_size = lax.axis_size("row"), lax.axis_size("col")
    count = atoms.shape[0]
    query_rows, width = single.shape
    head_rows = token_wo.shape[0]
    both = ("row", "col")
    devices = row_size * col_size
    up = [(i, i + 1) for i in range(devices - 1)]
    down = [(j, i) for i, j in up]
    before = lax.ppermute(atoms, both, up)
    after = lax.ppermute(atoms, both, down)

    device = lax.axis_index(both)
    place = jnp.stack(
        [
            device,
            lax.axis_index("row") * query_rows,
            jnp.asarray(count * devices, device.dtype),
            lax.axis_index("col"),
            lax.axis_index("row"),
        ]
    ).astype(jnp.int32)
    smem = pl.BlockSpec(memory_space=pltpu.SMEM)
    vmem = pl.BlockSpec(memory_space=pltpu.VMEM)
    token_row = atom_token.reshape(1, count)

    units = trans_in.shape[2]
    bias, done, win, wout = pair_call(
        pair_first, pair, (trans_in, trans_out, bias_w.T), 0, FIRST_ROWS, (),
        (shape(2 * units, CZ), shape(CZ, units)),
    )
    mid, mid_send, done = single_step(
        atom_kernel,
        "atom_stage",
        [vmem, smem] + [vmem] * 10,
        [shape(count, CA), shape(col_size, count + 16 + 2 * head_rows, CA), DONE],
        4_000_000_000,
        2_000_000,
        (
            done, place, before, atoms, after, atom_pair, atom_pair_w.T, token_row, atom_w, atom_wo, token_wo, back_w,
        ),
    )
    mids = gathered(mid_send, "col")
    bias, done = pair_call(pair_rest, pair, (win, wout, bias_w.T), FIRST_ROWS, query_rows, (bias, done), ())
    bias_rows = gathered(bias, "col")

    turned = jnp.transpose(token_w, (1, 2, 0)).reshape(4 * HEAD, width)
    token_in, held, kv_send = single_step(
        token_kernel,
        "token_stage",
        [vmem] * 6,
        [
            shape(query_rows, width),
            shape(HEAD, 2 * query_rows + CA),
            shape(2 * HEAD, query_rows),
        ],
        4_000_000_000,
        2_000_000,
        (done, mids, single, agg_w, turned, token_wo),
    )
    kv = [kv_send] + [
        lax.ppermute(kv_send, "row", [(i, (i + step) % row_size) for i in range(row_size)])
        for step in range(1, row_size)
    ]
    gated_send, done = single_step(
        attention_kernel,
        "token_attention",
        [smem] + [vmem] * (2 + row_size),
        [shape(col_size, HEAD, query_rows + CA), DONE],
        3_000_000_000,
        2_000_000,
        (place, held, bias_rows, *kv),
    )
    gated = gathered(gated_send, "col")
    out_w, own, back, onehot = single_step(
        ready_kernel,
        "out_ready",
        [vmem, smem] + [vmem] * 3,
        [
            shape(width // col_size, width),
            shape(width // col_size, query_rows, dtype=f32),
            shape(CA, query_rows, dtype=f32),
            shape(count, query_rows),
        ],
        2_000_000_000,
        2_000_000,
        (done, place, mids, token_in, token_row),
    )
    single_out, atoms_out = single_step(
        final_kernel,
        "token_out",
        [vmem] * 6,
        [shape(width // col_size, query_rows), shape(count, CA)],
        2_000_000_000,
        2_000_000,
        (gated, out_w, own, back, onehot, mid),
    )
    return single_out.T, atoms_out


def solution(mesh):
    in_specs = (
        P(("row", "col"), None),
        P(("row", "col"), None, None, None),
        P(("row", "col")),
        P("row", None),
        P("row", "col", None),
        P(),
        P(),
        P(),
        P(),
        P(),
        P(),
        P(),
        P(None, None, "col"),
        P("col", None),
        P("col", None),
    )
    out_specs = (P("row", "col"), P(("row", "col"), None))
    return jax.shard_map(body, mesh=mesh, in_specs=in_specs, out_specs=out_specs, check_vma=False)
```

```python
import functools
import math

import jax
import jax.numpy as jnp
from jax import lax
from jax.experimental import pallas as pl
from jax.experimental.pallas import tpu as pltpu
from jax.sharding import PartitionSpec as P

HEADS = 16
HEAD = 48
CA = 128
CZ = 128
ATOM_HEADS = 4
ATOM_HEAD = 32
QW = 32
KW = 128
RIM = (KW - QW) // 2
CORES = 2
PAIR_ROWS = 32
STREAMS = 1
FIRST_ROWS = 32
MIB = 2**20
DONE = jax.ShapeDtypeStruct((8, 128), jnp.float32)

epsilon = 1e-05
masked_score = -1e30
bf16 = jnp.bfloat16
f32 = jnp.float32


def dot(a, b):
    return jnp.dot(a, b, preferred_element_type=f32)


def dot_t(a, b):
    return lax.dot_general(a, b, (((1,), (1,)), ((), ())), preferred_element_type=f32)


def layer_norm(values):
    centred = values - jnp.mean(values, axis=-1, keepdims=True)
    spread = jnp.mean(centred * centred, axis=-1, keepdims=True)
    return centred * lax.rsqrt(spread + epsilon)


def params(mib=24):
    return pltpu.CompilerParams(vmem_limit_bytes=mib * MIB)


def cost(flops, moved):
    return pl.CostEstimate(flops=flops, bytes_accessed=moved, transcendentals=0)


def atom_kernel(
    first_ref, place_ref, before_ref, own_ref, after_ref, atom_pair_ref, pair_w_ref, token_ref, w_ref, wo_ref, out_w_ref,
    back_w_ref, mid_ref, send_ref, done_ref,
):
    done_ref[...] = jnp.zeros_like(done_ref)
    device, row, last = place_ref[0], place_ref[1], place_ref[2]
    atoms = own_ref[...].astype(f32)
    count = atoms.shape[0]
    extended = jnp.concatenate(
        [before_ref[count - RIM :, :].astype(f32), atoms, after_ref[:RIM, :].astype(f32)], axis=0
    )
    norm = layer_norm(extended).astype(bf16)
    wide = w_ref[...].astype(f32)
    query_all, key_all, value_all, gate_all = [dot(norm, wide[:, m, :].astype(bf16)).astype(bf16) for m in range(4)]
    lanes = lax.broadcasted_iota(jnp.int32, (1, CA), 1) // ATOM_HEAD
    keys = lax.broadcasted_iota(jnp.int32, (1, KW), 1)
    mix = pair_w_ref[...].astype(f32)
    parts = []
    for window in range(count // QW):
        start = window * QW
        query = query_all[RIM + start : RIM + start + QW]
        query = jnp.concatenate(
            [jnp.where(lanes == head, query, jnp.zeros_like(query)) for head in range(ATOM_HEADS)], axis=0
        )
        key = key_all[start : start + KW]
        value = value_all[start : start + KW]
        planes = [atom_pair_ref[window, c].astype(f32) for c in range(atom_pair_ref.shape[1])]
        bias = []
        for head in range(ATOM_HEADS):
            total = planes[0] * mix[head : head + 1, 0:1]
            for c in range(1, len(planes)):
                total = total + planes[c] * mix[head : head + 1, c : c + 1]
            bias.append(total)
        scores = dot_t(query, key) / math.sqrt(ATOM_HEAD) + jnp.concatenate(bias, axis=0)
        position = device * count - RIM + start + keys
        scores = jnp.where((position >= 0) & (position < last), scores, masked_score)
        raised = jnp.exp(scores - jnp.max(scores, axis=-1, keepdims=True))
        weights = (raised / jnp.sum(raised, axis=-1, keepdims=True)).astype(bf16)
        mixed = dot(weights, value)
        out = jnp.zeros((QW, CA), f32)
        for head in range(ATOM_HEADS):
            out = out + jnp.where(lanes == head, mixed[head * QW : (head + 1) * QW], 0.0)
        parts.append(out)
    attended = jnp.concatenate(parts, axis=0)
    gate = gate_all[RIM : RIM + count].astype(f32)
    gated = (jax.nn.sigmoid(gate) * attended).astype(bf16)
    mid = (atoms + dot(gated, wo_ref[...])).astype(bf16)
    mid_ref[...] = mid
    local = (token_ref[...] - row).astype(f32).astype(bf16)
    tail = jnp.broadcast_to(local, (16, count))
    back_w = back_w_ref[...]
    rows, width = out_w_ref.shape
    targets = send_ref.shape[0]
    mine = width // targets
    out_w = out_w_ref[...].astype(f32)
    blank = jnp.zeros((rows, CA - mine), bf16)
    for target in range(targets):
        part = out_w[:, target * mine : (target + 1) * mine].astype(bf16)
        pieces = [first_ref[target], mid, tail, back_w, jnp.concatenate([part, blank], axis=1)]
        start = 0
        for piece in pieces:
            send_ref[target, start : start + piece.shape[0], :] = piece
            start += piece.shape[0]


def pair_body(pair_refs, win_ref, wout_ref, wb_ref, out_ref, hold_ref):
    part, width, _ = pair_refs[0].shape
    rows = part * len(pair_refs)
    tile = jnp.concatenate([ref[...].reshape(part * width, CZ) for ref in pair_refs], axis=0)
    centred = dot_t(centre(), tile)
    spread = jnp.sum(centred * centred, axis=0, keepdims=True) * (1.0 / CZ)
    normed = (centred * lax.rsqrt(spread + epsilon)).astype(bf16)
    both = dot(win_ref[...], normed)
    half = both.shape[0] // 2
    gate, up = both[:half], both[half:]
    hidden = ((gate * jnp.tanh(gate) + gate) * up).astype(bf16)
    renewed = centred + dot(wout_ref[...], hidden)
    spread = jnp.sum(renewed * renewed, axis=0, keepdims=True) * (1.0 / CZ)
    bias = dot(wb_ref[...], renewed.astype(bf16)) * lax.rsqrt(spread + epsilon)
    for i in range(rows):
        hold_ref[:, i, :] = bias[:, i * width : (i + 1) * width]
    out_ref[...] = hold_ref[...].astype(bf16)


def centre():
    row = lax.broadcasted_iota(jnp.int32, (CZ, CZ), 0)
    column = lax.broadcasted_iota(jnp.int32, (CZ, CZ), 1)
    return (jnp.where(row == column, 1.0, 0.0) - 1.0 / CZ).astype(bf16)


def pair_first(*refs):
    *pair_refs, trans_in_ref, trans_out_ref, wb_ref, out_ref, done_ref, win_ref, wout_ref, hold_ref = refs

    @pl.when(pl.program_id(0) == 0)
    def _():
        wide = trans_in_ref[...].astype(f32)
        units = wide.shape[2]
        win_ref[:units, :] = (wide[:, 0, :].T * 0.5).astype(bf16)
        win_ref[units:, :] = wide[:, 1, :].T.astype(bf16)
        wout_ref[...] = dot_t(centre(), trans_out_ref[...]).astype(bf16)

    pair_body(pair_refs, win_ref, wout_ref, wb_ref, out_ref, hold_ref)
    done_ref[...] = jnp.zeros_like(done_ref)


def pair_rest(_, *refs):
    *pair_refs, win_ref, wout_ref, wb_ref, out_ref, done_ref, hold_ref = refs
    pair_body(pair_refs, win_ref, wout_ref, wb_ref, out_ref, hold_ref)
    done_ref[...] = jnp.zeros_like(done_ref)


def pair_call(kernel, pair, weights, start, stop, before, out_weights, mib):
    steps = (stop - start) // PAIR_ROWS
    vmem = pl.BlockSpec(memory_space=pltpu.VMEM)
    skip = start // PAIR_ROWS
    cols = pair.shape[1]
    in_specs = [vmem] * len(before)
    part = PAIR_ROWS // STREAMS
    in_specs += [
        pl.BlockSpec((part, cols, CZ), lambda i, k=k: ((i + skip) * STREAMS + k, 0, 0)) for k in range(STREAMS)
    ]
    in_specs += [vmem] * len(weights)
    positions = (stop - start) * cols
    return pl.pallas_call(
        kernel,
        grid=(steps,),
        in_specs=in_specs,
        out_specs=[pl.BlockSpec((HEADS, PAIR_ROWS, cols), lambda i: (0, i, 0))]
        + [vmem] * (1 + len(out_weights)),
        out_shape=[jax.ShapeDtypeStruct((HEADS, stop - start, cols), bf16), DONE, *out_weights],
        scratch_shapes=[pltpu.VMEM((HEADS, PAIR_ROWS, cols), f32)],
        compiler_params=params(mib),
        cost_estimate=cost(positions * 620_000, positions * 288),
        name="pair_bias",
    )(*before, *[pair] * STREAMS, *weights)


def token_kernel(
    _, got_ref, single_ref, agg_ref, w_ref, in_ref, held_ref, send_ref
):
    sources, count = got_ref.shape[0], got_ref.shape[2]
    tokens = single_ref.shape[0]
    first, ids = FIRST_ROWS, FIRST_ROWS + count
    mids = jnp.concatenate([got_ref[s, first:ids, :] for s in range(sources)], axis=0)
    features = jnp.maximum(dot(mids, agg_ref[...]), 0.0).astype(bf16)
    token = lax.broadcasted_iota(jnp.int32, (tokens, count), 0).astype(f32)
    onehot = jnp.concatenate(
        [
            jnp.where(token == got_ref[s, ids : ids + 16, :].astype(f32)[:1], 1.0, 0.0)
            for s in range(sources)
        ],
        axis=1,
    )
    token_count = jnp.sum(onehot, axis=1, keepdims=True)
    token_sum = dot(onehot.astype(bf16), features)
    token_in = (single_ref[...].astype(f32) + token_sum / token_count).astype(bf16)
    in_ref[...] = token_in
    norm = layer_norm(token_in.astype(f32)).astype(bf16)
    turned = dot_t(w_ref[...], norm).astype(bf16)
    held_ref[:, :tokens] = turned[:HEAD]
    held_ref[:, tokens:] = turned[3 * HEAD :]
    send_ref[...] = turned[HEAD : 3 * HEAD]


def hops_of(rows):
    hops = rows // CORES
    return sorted(range(hops), key=lambda hop: -min(hop, hops - hop) if hop else -hops)


def partner(row, rows, hop, cross):
    hops = rows // CORES
    chip, core = row // CORES, row % CORES
    return (chip + hop + hops) % hops * CORES + (core + cross) % CORES


def chip_kernel(own_ref, other_ref, out_ref):
    rows = own_ref.shape[0]
    out_ref[:rows, :] = own_ref[...]
    out_ref[rows:, :] = other_ref[...]


def attention_kernel(place_ref, held_ref, mixed_ref, got_ref, bias_ref, *refs):
    *kv_refs, send_ref = refs
    rows = len(kv_refs) * CORES
    tokens = kv_refs[0].shape[1]
    query = held_ref[:, :tokens].astype(f32).T.astype(bf16)
    per = bias_ref.shape[0] // rows
    scores, values = [], []
    for hop, kv_ref in zip(hops_of(rows), kv_refs):
        for cross in range(CORES):
            source = partner(place_ref[4], rows, -hop, cross) * per
            bias = jnp.concatenate(
                [
                    jnp.concatenate([got_ref[source + k, :FIRST_ROWS, :], bias_ref[source + k]], axis=0)
                    for k in range(per)
                ],
                axis=1,
            ).astype(f32)
            start = cross * 2 * HEAD
            scores.append(dot(query, kv_ref[start : start + HEAD, :]) / math.sqrt(HEAD) + bias)
            values.append(kv_ref[start + HEAD : start + 2 * HEAD, :])
    scores = jnp.concatenate(scores, axis=1)
    raised = jnp.exp(scores - jnp.max(scores, axis=-1, keepdims=True))
    weights = (raised / jnp.sum(raised, axis=-1, keepdims=True)).astype(bf16)
    values = jnp.concatenate(values, axis=1)
    attended = dot_t(values, weights)
    gate = held_ref[:, tokens:].astype(f32)
    gated = (jax.nn.sigmoid(gate) * attended).astype(bf16)
    back = mixed_ref[...]
    for target in range(send_ref.shape[0]):
        send_ref[target, :, :tokens] = gated
        send_ref[target, :, tokens:] = back


def ready_kernel(
    place_ref, got_ref, in_ref, token_ref, mine_ref, out_w_ref, own_ref, back_ref, onehot_ref, mixed_ref
):
    sources, count = got_ref.shape[0], got_ref.shape[2]
    tokens, width = in_ref.shape
    mine = width // sources
    token_in = in_ref[...]
    start = FIRST_ROWS + count + 16
    back_w = jnp.concatenate([got_ref[s, start : start + mine, :] for s in range(sources)], axis=0)
    out_w = jnp.concatenate([got_ref[s, start + mine :, :] for s in range(sources)], axis=0)
    mixed_ref[...] = dot(mine_ref[...], back_w).astype(bf16)
    out_w_ref[...] = out_w.astype(f32).T[:mine].astype(bf16)
    back_ref[...] = dot_t(back_w.astype(f32).T.astype(bf16), token_in)
    wanted = lax.broadcasted_iota(jnp.int32, (mine, width), 0) + place_ref[3] * mine
    column = lax.broadcasted_iota(jnp.int32, (mine, width), 1)
    own_ref[...] = dot_t(jnp.where(column == wanted, 1.0, 0.0).astype(bf16), token_in)
    token = lax.broadcasted_iota(jnp.int32, (tokens, count), 0)
    onehot = jnp.where(token == token_ref[...] - place_ref[1], 1.0, 0.0)
    onehot_ref[...] = onehot.T.astype(bf16)


def final_kernel(got_ref, out_w_ref, own_ref, back_ref, onehot_ref, mid_ref, single_ref, atoms_ref):
    heads, head, _ = got_ref.shape
    tokens = own_ref.shape[1]
    gated = got_ref[:, :, :tokens].reshape(heads * head, tokens)
    mixed = got_ref[:, :, tokens:].reshape(heads * head, CA)
    single_ref[...] = (own_ref[...] + dot(out_w_ref[...], gated)).astype(bf16)
    back = (back_ref[...] + dot(mixed.astype(f32).T.astype(bf16), gated)).astype(bf16)
    picked = dot_t(onehot_ref[...], back)
    atoms_ref[...] = (mid_ref[...].astype(f32) + picked).astype(bf16)


def shape(*sizes, dtype=bf16):
    return jax.ShapeDtypeStruct(sizes, dtype)


def single_step(kernel, name, in_specs, out_shape, flops, moved, operands):
    return pl.pallas_call(
        kernel,
        in_specs=in_specs,
        out_specs=[pl.BlockSpec(memory_space=pltpu.VMEM)] * len(out_shape),
        out_shape=out_shape,
        compiler_params=params(),
        cost_estimate=cost(flops, moved),
        name=name,
    )(*operands)


def gathered(copies, axis):
    return lax.all_to_all(copies, axis, split_axis=0, concat_axis=0, tiled=True)


def body(
    atoms,
    atom_pair,
    atom_token,
    single,
    pair,
    atom_w,
    atom_pair_w,
    atom_wo,
    agg_w,
    trans_in,
    trans_out,
    bias_w,
    token_w,
    token_wo,
    back_w,
):
    row_size, col_size = lax.axis_size("row"), lax.axis_size("col")
    count = atoms.shape[0]
    query_rows, width = single.shape
    head_rows = token_wo.shape[0]
    both = ("row", "col")
    devices = row_size * col_size
    up = [(i, i + 1) for i in range(devices - 1)]
    down = [(j, i) for i, j in up]
    before = lax.ppermute(atoms, both, up)
    after = lax.ppermute(atoms, both, down)

    device = lax.axis_index(both)
    place = jnp.stack(
        [
            device,
            lax.axis_index("row") * query_rows,
            jnp.asarray(count * devices, device.dtype),
            lax.axis_index("col"),
            lax.axis_index("row"),
        ]
    ).astype(jnp.int32)
    smem = pl.BlockSpec(memory_space=pltpu.SMEM)
    vmem = pl.BlockSpec(memory_space=pltpu.VMEM)
    token_row = atom_token.reshape(1, count)

    units = trans_in.shape[2]
    first_bias, _, win, wout = pair_call(
        pair_first, pair, (trans_in, trans_out, bias_w.T), 0, FIRST_ROWS, (),
        (shape(2 * units, CZ), shape(CZ, units)), 56,
    )
    mid, mid_send, done = single_step(
        atom_kernel,
        "atom_stage",
        [vmem, smem] + [vmem] * 10,
        [shape(count, CA), shape(col_size, FIRST_ROWS + count + 16 + 2 * head_rows, CA), DONE],
        4_000_000_000,
        2_000_000,
        (
            first_bias, place, before, atoms, after, atom_pair, atom_pair_w.T, token_row, atom_w, atom_wo, token_wo, back_w,
        ),
    )
    mids = gathered(mid_send, "col")
    bias, done = pair_call(pair_rest, pair, (win, wout, bias_w.T), FIRST_ROWS, query_rows, (done,), (), 52)
    bias_rows = gathered(bias, "col")

    turned = jnp.transpose(token_w, (1, 2, 0)).reshape(4 * HEAD, width)
    token_in, held, kv_send = single_step(
        token_kernel,
        "token_stage",
        [vmem] * 5,
        [
            shape(query_rows, width),
            shape(HEAD, 2 * query_rows),
            shape(2 * HEAD, query_rows),
        ],
        4_000_000_000,
        2_000_000,
        (done, mids, single, agg_w, turned),
    )
    across = lax.ppermute(kv_send, "row", [(i, partner(i, row_size, 0, 1)) for i in range(row_size)])
    (chip_kv,) = single_step(
        chip_kernel,
        "chip_keys",
        [vmem] * 2,
        [shape(4 * HEAD, query_rows)],
        1_000_000,
        200_000,
        (kv_send, across),
    )
    kv = [chip_kv] + [
        lax.ppermute(chip_kv, "row", [(i, partner(i, row_size, hop, 0)) for i in range(row_size)])
        for hop in hops_of(row_size)[1:]
    ]
    out_w, own, back, onehot, mixed = single_step(
        ready_kernel,
        "out_ready",
        [smem] + [vmem] * 4,
        [
            shape(width // col_size, width),
            shape(width // col_size, query_rows, dtype=f32),
            shape(CA, query_rows, dtype=f32),
            shape(count, query_rows),
            shape(head_rows, CA),
        ],
        2_000_000_000,
        2_000_000,
        (place, mids, token_in, token_row, token_wo),
    )
    (gated_send,) = single_step(
        attention_kernel,
        "token_attention",
        [smem] + [vmem] * (4 + len(kv)),
        [shape(col_size, HEAD, query_rows + CA)],
        3_000_000_000,
        2_000_000,
        (place, held, mixed, mids, bias_rows, *kv),
    )
    gated = gathered(gated_send, "col")
    single_out, atoms_out = single_step(
        final_kernel,
        "token_out",
        [vmem] * 6,
        [shape(width // col_size, query_rows), shape(count, CA)],
        2_000_000_000,
        2_000_000,
        (gated, out_w, own, back, onehot, mid),
    )
    return single_out.T, atoms_out


def solution(mesh):
    in_specs = (
        P(("row", "col"), None),
        P(("row", "col"), None, None, None),
        P(("row", "col")),
        P("row", None),
        P("row", "col", None),
        P(),
        P(),
        P(),
        P(),
        P(),
        P(),
        P(),
        P(None, None, "col"),
        P("col", None),
        P("col", None),
    )
    out_specs = (P("row", "col"), P(("row", "col"), None))
    return jax.shard_map(body, mesh=mesh, in_specs=in_specs, out_specs=out_specs, check_vma=False)
```

```python
import functools
import math

import jax
import jax.numpy as jnp
from jax import lax
from jax.experimental import pallas as pl
from jax.experimental.pallas import tpu as pltpu
from jax.sharding import PartitionSpec as P

HEADS = 16
HEAD = 48
CA = 128
CZ = 128
ATOM_HEADS = 4
ATOM_HEAD = 32
QW = 32
KW = 128
RIM = (KW - QW) // 2
CORES = 2
PAIR_ROWS = 32
FIRST_ROWS = 32
EARLY_ROWS = 64
MIB = 2**20
DONE = jax.ShapeDtypeStruct((8, 128), jnp.float32)

epsilon = 1e-05
masked_score = -1e30
bf16 = jnp.bfloat16
f32 = jnp.float32


def dot(a, b):
    return jnp.dot(a, b, preferred_element_type=f32)


def dot_t(a, b):
    return lax.dot_general(a, b, (((1,), (1,)), ((), ())), preferred_element_type=f32)


def layer_norm(values):
    centred = values - jnp.mean(values, axis=-1, keepdims=True)
    spread = jnp.mean(centred * centred, axis=-1, keepdims=True)
    return centred * lax.rsqrt(spread + epsilon)


def params(mib=24):
    return pltpu.CompilerParams(vmem_limit_bytes=mib * MIB)


def in_hbm(array):
    return pltpu.with_memory_space_constraint(array, pltpu.HBM)


def cost(flops, moved):
    return pl.CostEstimate(flops=flops, bytes_accessed=moved, transcendentals=0)


def regrouped(size, groups):
    row = lax.broadcasted_iota(jnp.int32, (size, size), 0)
    column = lax.broadcasted_iota(jnp.int32, (size, size), 1)
    length = size // groups
    return jnp.where(column == (row % length) * groups + row // length, 1.0, 0.0).astype(bf16)


def atom_kernel(
    first_ref, place_ref, even_ref, own_ref, odd_ref, atom_pair_ref, pair_w_ref, token_ref, w_ref, wo_ref,
    out_w_ref, back_w_ref, send_ref, mid_ref, done_ref, hold_ref, slice_ref, block_sem, hold_sem, back_sem,
):
    done_ref[...] = jnp.zeros_like(done_ref)
    device, row, last = place_ref[0], place_ref[1], place_ref[2]
    atoms = own_ref[...].astype(f32)
    count = atoms.shape[0]
    odd = device % 2 == 1
    before = jnp.where(odd, even_ref[count - RIM :, :].astype(f32), odd_ref[count - RIM :, :].astype(f32))
    after = jnp.where(odd, odd_ref[:RIM, :].astype(f32), even_ref[:RIM, :].astype(f32))
    extended = jnp.concatenate([before, atoms, after], axis=0)
    norm = layer_norm(extended).astype(bf16)
    sorted_w = dot(regrouped(4 * CA, 4), w_ref[...]).astype(bf16)
    query_all, key_all, value_all, gate_all = [
        dot(norm, sorted_w[m * CA : (m + 1) * CA]).astype(bf16) for m in range(4)
    ]
    targets = send_ref.shape[0]
    rows, width = out_w_ref.shape
    mine = width // targets
    half = rows // 2
    start = FIRST_ROWS + count
    out_w = out_w_ref[...].astype(f32)
    local = (token_ref[...] - row).astype(f32)
    spare = jnp.zeros((half, CA // 2 - mine), f32)
    for target in range(targets):
        part = out_w[:, target * mine : (target + 1) * mine]
        packed = jnp.concatenate([part[:half], spare, part[half:], spare], axis=1)
        slice_ref[target] = jnp.concatenate([packed, jnp.broadcast_to(local, (8, CA))], axis=0).astype(bf16)
    early = [
        pltpu.make_async_copy(
            first_ref.at[:, pl.ds(0, FIRST_ROWS), :], send_ref.at[:, pl.ds(0, FIRST_ROWS), :], block_sem.at[0]
        ),
        pltpu.make_async_copy(slice_ref, send_ref.at[:, pl.ds(start + rows, half + 8), :], block_sem.at[1]),
    ]
    early += [
        pltpu.make_async_copy(back_w_ref, send_ref.at[target, pl.ds(start, rows), :], back_sem.at[target])
        for target in range(targets)
    ]
    for copy in early:
        copy.start()
    lanes = lax.broadcasted_iota(jnp.int32, (1, CA), 1) // ATOM_HEAD
    keys = lax.broadcasted_iota(jnp.int32, (1, KW), 1)
    mix = pair_w_ref[...].astype(f32)
    parts = []
    for window in range(count // QW):
        start = window * QW
        query = query_all[RIM + start : RIM + start + QW]
        query = jnp.concatenate(
            [jnp.where(lanes == head, query, jnp.zeros_like(query)) for head in range(ATOM_HEADS)], axis=0
        )
        key = key_all[start : start + KW]
        value = value_all[start : start + KW]
        planes = [atom_pair_ref[window, c].astype(f32) for c in range(atom_pair_ref.shape[1])]
        bias = []
        for head in range(ATOM_HEADS):
            total = planes[0] * mix[head : head + 1, 0:1]
            for c in range(1, len(planes)):
                total = total + planes[c] * mix[head : head + 1, c : c + 1]
            bias.append(total)
        scores = dot_t(query, key) / math.sqrt(ATOM_HEAD) + jnp.concatenate(bias, axis=0)
        position = device * count - RIM + start + keys
        scores = jnp.where((position >= 0) & (position < last), scores, masked_score)
        raised = jnp.exp(scores - jnp.max(scores, axis=-1, keepdims=True))
        weights = (raised / jnp.sum(raised, axis=-1, keepdims=True)).astype(bf16)
        mixed = dot(weights, value)
        out = jnp.zeros((QW, CA), f32)
        for head in range(ATOM_HEADS):
            out = out + jnp.where(lanes == head, mixed[head * QW : (head + 1) * QW], 0.0)
        parts.append(out)
    attended = jnp.concatenate(parts, axis=0)
    gate = gate_all[RIM : RIM + count].astype(f32)
    gated = (jax.nn.sigmoid(gate) * attended).astype(bf16)
    mid = (atoms + dot(gated, wo_ref[...])).astype(bf16)
    mid_ref[...] = mid
    hold_ref[...] = mid
    late = [
        pltpu.make_async_copy(hold_ref, send_ref.at[target, pl.ds(FIRST_ROWS, count), :], hold_sem.at[target])
        for target in range(targets)
    ]
    for copy in late:
        copy.start()
    for copy in early + late:
        copy.wait()


def pair_body(pair_refs, win_ref, wout_ref, wb_ref, hold_ref):
    part, width, _ = pair_refs[0].shape
    rows = part * len(pair_refs)
    tile = jnp.concatenate([ref[...].reshape(part * width, CZ) for ref in pair_refs], axis=0)
    centred = dot_t(centre(), tile)
    spread = jnp.sum(centred * centred, axis=0, keepdims=True) * (1.0 / CZ)
    normed = (centred * lax.rsqrt(spread + epsilon)).astype(bf16)
    both = dot(win_ref[...], normed)
    half = both.shape[0] // 2
    gate, up = both[:half], both[half:]
    hidden = ((gate * jnp.tanh(gate) + gate) * up).astype(bf16)
    renewed = centred + dot(wout_ref[...], hidden)
    spread = jnp.sum(renewed * renewed, axis=0, keepdims=True) * (1.0 / CZ)
    bias = dot(wb_ref[...], renewed.astype(bf16)) * lax.rsqrt(spread + epsilon)
    for i in range(rows):
        hold_ref[:, i, :] = bias[:, i * width : (i + 1) * width]
    return hold_ref[...].astype(bf16)


def centre():
    row = lax.broadcasted_iota(jnp.int32, (CZ, CZ), 0)
    column = lax.broadcasted_iota(jnp.int32, (CZ, CZ), 1)
    return (jnp.where(row == column, 1.0, 0.0) - 1.0 / CZ).astype(bf16)


def pair_first(*refs):
    *pair_refs, trans_in_ref, trans_out_ref, wb_ref, out_ref, win_ref, wout_ref, hold_ref = refs

    @pl.when(pl.program_id(0) == 0)
    def _():
        units = win_ref.shape[0] // 2
        parts = units // CZ
        wide = dot(regrouped(win_ref.shape[0], 2 * parts), trans_in_ref[...])
        for part in range(parts):
            gate = wide[2 * part * CZ : (2 * part + 1) * CZ]
            up = wide[(2 * part + 1) * CZ : (2 * part + 2) * CZ]
            win_ref[part * CZ : (part + 1) * CZ, :] = (gate.T * 0.5).astype(bf16)
            win_ref[units + part * CZ : units + (part + 1) * CZ, :] = up.T.astype(bf16)
        wout_ref[...] = dot_t(centre(), trans_out_ref[...]).astype(bf16)

    rows = pl.ds(pl.multiple_of(pl.program_id(0) * PAIR_ROWS, PAIR_ROWS), PAIR_ROWS)
    out_ref[:, rows, :] = pair_body(pair_refs, win_ref, wout_ref, wb_ref, hold_ref)


def pair_rest(_, early_ref, *refs):
    *pair_refs, win_ref, wout_ref, wb_ref, out_ref, done_ref, hold_ref = refs
    done_ref[...] = jnp.zeros_like(done_ref)

    @pl.when(pl.program_id(0) == 0)
    def _():
        out_ref[...] = early_ref[:, FIRST_ROWS:, :]

    @pl.when(pl.program_id(0) > 0)
    def _():
        out_ref[...] = pair_body(pair_refs, win_ref, wout_ref, wb_ref, hold_ref)


def pair_call(kernel, pair, before, weights, steps, block, out_specs, out_shape):
    cols = pair.shape[1]
    vmem = pl.BlockSpec(memory_space=pltpu.VMEM)
    positions = steps * PAIR_ROWS * cols
    return pl.pallas_call(
        kernel,
        grid=(steps,),
        in_specs=[vmem] * len(before)
        + [pl.BlockSpec((PAIR_ROWS, cols, CZ), lambda i: (block(i), 0, 0))]
        + [vmem] * len(weights),
        out_specs=out_specs,
        out_shape=out_shape,
        scratch_shapes=[pltpu.VMEM((HEADS, PAIR_ROWS, cols), f32)],
        compiler_params=params(48),
        cost_estimate=cost(positions * 620_000, positions * 288),
        name="pair_bias",
    )(*before, in_hbm(pair), *weights)


def token_kernel(
    _, got_ref, single_ref, agg_ref, w_ref, in_ref, held_ref, send_ref
):
    sources, count = got_ref.shape[0], got_ref.shape[2]
    tokens = single_ref.shape[0]
    first, ids = FIRST_ROWS, FIRST_ROWS + count
    mids = jnp.concatenate([got_ref[s, first:ids, :] for s in range(sources)], axis=0)
    features = jnp.maximum(dot(mids, agg_ref[...]), 0.0).astype(bf16)
    token = lax.broadcasted_iota(jnp.int32, (tokens, count), 0).astype(f32)
    onehot = jnp.concatenate(
        [
            jnp.where(token == got_ref[s, ids + HEAD + HEAD // 2 - 8 :, :].astype(f32)[8:9], 1.0, 0.0)
            for s in range(sources)
        ],
        axis=1,
    )
    token_count = jnp.sum(onehot, axis=1, keepdims=True)
    token_sum = dot(onehot.astype(bf16), features)
    token_in = (single_ref[...].astype(f32) + token_sum / token_count).astype(bf16)
    in_ref[...] = token_in
    norm = layer_norm(token_in.astype(f32)).astype(bf16)
    turned = dot_t(w_ref[...], norm).astype(bf16)
    held_ref[:, :tokens] = turned[:HEAD]
    held_ref[:, tokens:] = turned[3 * HEAD :]
    send_ref[...] = turned[HEAD : 3 * HEAD]


def partner(row, hop, cross):
    return (row // CORES ^ hop) * CORES + (row % CORES ^ cross)


def chip_kernel(own_ref, other_ref, out_ref):
    rows = own_ref.shape[0]
    out_ref[:rows, :] = own_ref[...]
    out_ref[rows:, :] = other_ref[...]


def attention_kernel(place_ref, held_ref, mixed_ref, got_ref, bias_ref, *refs):
    *kv_refs, send_ref = refs
    rows = len(kv_refs) * CORES
    tokens = kv_refs[0].shape[1]
    query = held_ref[:, :tokens].astype(f32).T.astype(bf16)
    per = bias_ref.shape[0] // rows
    scores, values = [], []
    for hop, kv_ref in enumerate(kv_refs):
        for cross in range(CORES):
            source = partner(place_ref[4], hop, cross) * per
            bias = jnp.concatenate(
                [
                    jnp.concatenate([got_ref[source + k, :FIRST_ROWS, :], bias_ref[source + k]], axis=0)
                    for k in range(per)
                ],
                axis=1,
            ).astype(f32)
            start = cross * 2 * HEAD
            scores.append(dot(query, kv_ref[start : start + HEAD, :]) / math.sqrt(HEAD) + bias)
            values.append(kv_ref[start + HEAD : start + 2 * HEAD, :])
    scores = jnp.concatenate(scores, axis=1)
    raised = jnp.exp(scores - jnp.max(scores, axis=-1, keepdims=True))
    weights = (raised / jnp.sum(raised, axis=-1, keepdims=True)).astype(bf16)
    values = jnp.concatenate(values, axis=1)
    attended = dot_t(values, weights)
    gate = held_ref[:, tokens:].astype(f32)
    gated = (jax.nn.sigmoid(gate) * attended).astype(bf16)
    back = mixed_ref[...]
    for target in range(send_ref.shape[0]):
        send_ref[target, :, :tokens] = gated
        send_ref[target, :, tokens:] = back


def ready_kernel(
    place_ref, got_ref, in_ref, token_ref, mine_ref, out_w_ref, own_ref, back_ref, onehot_ref, mixed_ref
):
    sources, count = got_ref.shape[0], got_ref.shape[2]
    tokens, width = in_ref.shape
    mine = width // sources
    token_in = in_ref[...]
    start = FIRST_ROWS + count
    back_w = jnp.concatenate([got_ref[s, start : start + mine, :] for s in range(sources)], axis=0)
    half = mine // 2
    packed = [got_ref[s, start + mine :, :].astype(f32)[:half] for s in range(sources)]
    out_w = jnp.concatenate(
        [jnp.concatenate([part, pltpu.roll(part, CA // 2, 1)], axis=0) for part in packed], axis=0
    )
    mixed_ref[...] = dot(mine_ref[...], back_w).astype(bf16)
    out_w_ref[...] = out_w.T[:mine].astype(bf16)
    back_ref[...] = dot_t(back_w.astype(f32).T.astype(bf16), token_in)
    wanted = lax.broadcasted_iota(jnp.int32, (mine, width), 0) + place_ref[3] * mine
    column = lax.broadcasted_iota(jnp.int32, (mine, width), 1)
    own_ref[...] = dot_t(jnp.where(column == wanted, 1.0, 0.0).astype(bf16), token_in)
    token = lax.broadcasted_iota(jnp.int32, (tokens, count), 0)
    onehot = jnp.where(token == token_ref[...] - place_ref[1], 1.0, 0.0)
    onehot_ref[...] = onehot.T.astype(bf16)


def final_kernel(got_ref, out_w_ref, own_ref, back_ref, onehot_ref, mid_ref, single_ref, atoms_ref):
    heads, head, _ = got_ref.shape
    tokens = own_ref.shape[1]
    gated = got_ref[:, :, :tokens].reshape(heads * head, tokens)
    mixed = got_ref[:, :, tokens:].reshape(heads * head, CA)
    single_ref[...] = (own_ref[...] + dot(out_w_ref[...], gated)).astype(bf16)
    back = (back_ref[...] + dot(mixed.astype(f32).T.astype(bf16), gated)).astype(bf16)
    picked = dot_t(onehot_ref[...], back)
    atoms_ref[...] = (mid_ref[...].astype(f32) + picked).astype(bf16)


def shape(*sizes, dtype=bf16):
    return jax.ShapeDtypeStruct(sizes, dtype)


def single_step(kernel, name, in_specs, out_shape, flops, moved, operands):
    return pl.pallas_call(
        kernel,
        in_specs=in_specs,
        out_specs=[pl.BlockSpec(memory_space=pltpu.VMEM)] * len(out_shape),
        out_shape=out_shape,
        compiler_params=params(),
        cost_estimate=cost(flops, moved),
        name=name,
    )(*operands)


def gathered(copies, axis):
    return lax.all_to_all(copies, axis, split_axis=0, concat_axis=0, tiled=True)


def body(
    atoms,
    atom_pair,
    atom_token,
    single,
    pair,
    atom_w,
    atom_pair_w,
    atom_wo,
    agg_w,
    trans_in,
    trans_out,
    bias_w,
    token_w,
    token_wo,
    back_w,
):
    row_size, col_size = lax.axis_size("row"), lax.axis_size("col")
    count = atoms.shape[0]
    query_rows, width = single.shape
    head_rows = token_wo.shape[0]
    both = ("row", "col")
    devices = row_size * col_size
    pairs = [[(i, i + 1) for i in range(start, devices - 1, 2)] for start in range(2)]
    swaps = [lax.ppermute(atoms, both, pair + [(j, i) for i, j in pair]) for pair in pairs]

    device = lax.axis_index(both)
    place = jnp.stack(
        [
            device,
            lax.axis_index("row") * query_rows,
            jnp.asarray(count * devices, device.dtype),
            lax.axis_index("col"),
            lax.axis_index("row"),
        ]
    ).astype(jnp.int32)
    smem = pl.BlockSpec(memory_space=pltpu.SMEM)
    vmem = pl.BlockSpec(memory_space=pltpu.VMEM)
    token_row = atom_token.reshape(1, count)

    units = trans_in.shape[2]
    trans_rows = trans_in.reshape(CZ, 2, units // CZ, CZ).transpose(0, 2, 1, 3).reshape(2 * units, CZ)
    key_cols = pair.shape[1]
    early, win, wout = pair_call(
        pair_first,
        pair,
        (),
        (in_hbm(trans_rows), in_hbm(trans_out), in_hbm(bias_w.T)),
        EARLY_ROWS // PAIR_ROWS,
        lambda i: i,
        [vmem] * 3,
        [shape(HEADS, EARLY_ROWS, key_cols), shape(2 * units, CZ), shape(CZ, units)],
    )
    misc = head_rows // 2 + 8
    mid_send, mid, done = pl.pallas_call(
        atom_kernel,
        in_specs=[vmem, smem] + [vmem] * 10,
        out_specs=[pl.BlockSpec(memory_space=pltpu.HBM), vmem, vmem],
        out_shape=[
            pltpu.HBM((col_size, FIRST_ROWS + count + head_rows + misc, CA), bf16),
            shape(count, CA),
            DONE,
        ],
        scratch_shapes=[
            pltpu.VMEM((count, CA), bf16),
            pltpu.VMEM((col_size, misc, CA), bf16),
            pltpu.SemaphoreType.DMA((2,)),
            pltpu.SemaphoreType.DMA((col_size,)),
            pltpu.SemaphoreType.DMA((col_size,)),
        ],
        compiler_params=params(),
        cost_estimate=cost(4_000_000_000, 2_000_000),
        name="atom_stage",
    )(early, place, swaps[0], atoms, swaps[1], atom_pair, atom_pair_w.T, token_row, atom_w.reshape(4 * CA, CA), atom_wo,
      token_wo, back_w)
    mids = gathered(mid_send, "col")
    late_rows = query_rows - FIRST_ROWS
    bias, done = pair_call(
        pair_rest,
        pair,
        (done, early),
        (win, wout, in_hbm(bias_w.T)),
        late_rows // PAIR_ROWS,
        lambda i: jnp.maximum(i, 1) + FIRST_ROWS // PAIR_ROWS,
        [pl.BlockSpec((HEADS, PAIR_ROWS, key_cols), lambda i: (0, i, 0)), vmem],
        [shape(HEADS, late_rows, key_cols), DONE],
    )
    bias_rows = gathered(bias, "col")

    turned = jnp.transpose(token_w, (1, 2, 0)).reshape(4 * HEAD, width)
    token_in, held, kv_send = single_step(
        token_kernel,
        "token_stage",
        [vmem] * 5,
        [
            shape(query_rows, width),
            shape(HEAD, 2 * query_rows),
            shape(2 * HEAD, query_rows),
        ],
        4_000_000_000,
        2_000_000,
        (done, mids, single, agg_w, turned),
    )
    across = lax.ppermute(kv_send, "row", [(i, partner(i, 0, 1)) for i in range(row_size)])
    (chip_kv,) = single_step(
        chip_kernel,
        "chip_keys",
        [vmem] * 2,
        [shape(4 * HEAD, query_rows)],
        1_000_000,
        200_000,
        (kv_send, across),
    )
    kv = [chip_kv] + [
        lax.ppermute(chip_kv, "row", [(i, partner(i, hop, 0)) for i in range(row_size)])
        for hop in range(1, row_size // CORES)
    ]
    out_w, own, back, onehot, mixed = single_step(
        ready_kernel,
        "out_ready",
        [smem] + [vmem] * 4,
        [
            shape(width // col_size, width),
            shape(width // col_size, query_rows, dtype=f32),
            shape(CA, query_rows, dtype=f32),
            shape(count, query_rows),
            shape(head_rows, CA),
        ],
        2_000_000_000,
        2_000_000,
        (place, mids, token_in, token_row, token_wo),
    )
    (gated_send,) = single_step(
        attention_kernel,
        "token_attention",
        [smem] + [vmem] * (4 + len(kv)),
        [shape(col_size, HEAD, query_rows + CA)],
        3_000_000_000,
        2_000_000,
        (place, held, mixed, mids, bias_rows, *kv),
    )
    gated = gathered(gated_send, "col")
    single_out, atoms_out = single_step(
        final_kernel,
        "token_out",
        [vmem] * 6,
        [shape(width // col_size, query_rows), shape(count, CA)],
        2_000_000_000,
        2_000_000,
        (gated, out_w, own, back, onehot, mid),
    )
    return single_out.T, atoms_out


def solution(mesh):
    in_specs = (
        P(("row", "col"), None),
        P(("row", "col"), None, None, None),
        P(("row", "col")),
        P("row", None),
        P("row", "col", None),
        P(),
        P(),
        P(),
        P(),
        P(),
        P(),
        P(),
        P(None, None, "col"),
        P("col", None),
        P("col", None),
    )
    out_specs = (P("row", "col"), P(("row", "col"), None))
    return jax.shard_map(body, mesh=mesh, in_specs=in_specs, out_specs=out_specs, check_vma=False)
```

```python
import functools
import math

import jax
import jax.numpy as jnp
from jax import lax
from jax.experimental import pallas as pl
from jax.experimental.pallas import tpu as pltpu
from jax.sharding import PartitionSpec as P

HEADS = 16
HEAD = 48
CA = 128
CZ = 128
ATOM_HEADS = 4
ATOM_HEAD = 32
QW = 32
KW = 128
RIM = (KW - QW) // 2
CORES = 2
COPIES = 4
PAIR_ROWS = 32
FIRST_ROWS = 32
EARLY_ROWS = 64
MIB = 2**20
DONE = jax.ShapeDtypeStruct((8, 128), jnp.float32)

epsilon = 1e-05
masked_score = -1e30
bf16 = jnp.bfloat16
f32 = jnp.float32


def dot(a, b):
    return jnp.dot(a, b, preferred_element_type=f32)


def dot_t(a, b):
    return lax.dot_general(a, b, (((1,), (1,)), ((), ())), preferred_element_type=f32)


def layer_norm(values):
    centred = values - jnp.mean(values, axis=-1, keepdims=True)
    spread = jnp.mean(centred * centred, axis=-1, keepdims=True)
    return centred * lax.rsqrt(spread + epsilon)


def params(mib=24):
    return pltpu.CompilerParams(vmem_limit_bytes=mib * MIB)


def in_hbm(array):
    return pltpu.with_memory_space_constraint(array, pltpu.HBM)


def cost(flops, moved):
    return pl.CostEstimate(flops=flops, bytes_accessed=moved, transcendentals=0)


def regrouped(rows, groups):
    row = lax.broadcasted_iota(jnp.int32, (CZ, CZ), 0)
    column = lax.broadcasted_iota(jnp.int32, (CZ, CZ), 1)
    length = CZ // groups
    order = jnp.where(column == (row % length) * groups + row // length, 1.0, 0.0).astype(bf16)
    blocks = [dot(order, rows[start : start + CZ]) for start in range(0, rows.shape[0], CZ)]
    return [
        jnp.concatenate([block[group * length : (group + 1) * length] for block in blocks], axis=0)
        for group in range(groups)
    ]


def atom_kernel(
    first_ref, place_ref, even_ref, own_ref, odd_ref, atom_pair_ref, pair_w_ref, token_ref, w_ref, wo_ref,
    out_w_ref, back_w_ref, send_ref, mid_ref, done_ref, hold_ref, slice_ref, block_sem, hold_sem,
):
    done_ref[...] = jnp.zeros_like(done_ref)
    device, row, last = place_ref[0], place_ref[1], place_ref[2]
    atoms = own_ref[...].astype(f32)
    count = atoms.shape[0]
    odd = device % 2 == 1
    before = jnp.where(odd, even_ref[count - RIM :, :].astype(f32), odd_ref[count - RIM :, :].astype(f32))
    after = jnp.where(odd, odd_ref[:RIM, :].astype(f32), even_ref[:RIM, :].astype(f32))
    extended = jnp.concatenate([before, atoms, after], axis=0)
    norm = layer_norm(extended).astype(bf16)
    query_all, key_all, value_all, gate_all = [
        dot(norm, part.astype(bf16)).astype(bf16) for part in regrouped(w_ref[...], 4)
    ]
    targets = send_ref.shape[0]
    rows, width = out_w_ref.shape
    mine = width // targets
    half = rows // 2
    start = FIRST_ROWS + count
    back_w = back_w_ref[...]
    out_w = out_w_ref[...].astype(f32)
    local = (token_ref[...] - row).astype(f32)
    spare = jnp.zeros((half, CA // 2 - mine), f32)
    for target in range(targets):
        part = out_w[:, target * mine : (target + 1) * mine]
        packed = jnp.concatenate([part[:half], spare, part[half:], spare], axis=1)
        slice_ref[target, :rows] = back_w
        slice_ref[target, rows:] = jnp.concatenate([packed, jnp.broadcast_to(local, (8, CA))], axis=0).astype(bf16)
    early = [
        pltpu.make_async_copy(
            first_ref.at[:, pl.ds(0, FIRST_ROWS), :], send_ref.at[:, pl.ds(0, FIRST_ROWS), :], block_sem.at[0]
        ),
        pltpu.make_async_copy(slice_ref, send_ref.at[:, pl.ds(start, rows + half + 8), :], block_sem.at[1]),
    ]
    for copy in early:
        copy.start()
    lanes = lax.broadcasted_iota(jnp.int32, (1, CA), 1) // ATOM_HEAD
    keys = lax.broadcasted_iota(jnp.int32, (1, KW), 1)
    mix = pair_w_ref[...].astype(f32)
    parts = []
    for window in range(count // QW):
        start = window * QW
        query = query_all[RIM + start : RIM + start + QW]
        query = jnp.concatenate(
            [jnp.where(lanes == head, query, jnp.zeros_like(query)) for head in range(ATOM_HEADS)], axis=0
        )
        key = key_all[start : start + KW]
        value = value_all[start : start + KW]
        planes = [atom_pair_ref[window, c].astype(f32) for c in range(atom_pair_ref.shape[1])]
        bias = []
        for head in range(ATOM_HEADS):
            total = planes[0] * mix[head : head + 1, 0:1]
            for c in range(1, len(planes)):
                total = total + planes[c] * mix[head : head + 1, c : c + 1]
            bias.append(total)
        scores = dot_t(query, key) / math.sqrt(ATOM_HEAD) + jnp.concatenate(bias, axis=0)
        position = device * count - RIM + start + keys
        scores = jnp.where((position >= 0) & (position < last), scores, masked_score)
        raised = jnp.exp(scores - jnp.max(scores, axis=-1, keepdims=True))
        weights = (raised / jnp.sum(raised, axis=-1, keepdims=True)).astype(bf16)
        mixed = dot(weights, value)
        out = jnp.zeros((QW, CA), f32)
        for head in range(ATOM_HEADS):
            out = out + jnp.where(lanes == head, mixed[head * QW : (head + 1) * QW], 0.0)
        parts.append(out)
    attended = jnp.concatenate(parts, axis=0)
    gate = gate_all[RIM : RIM + count].astype(f32)
    gated = (jax.nn.sigmoid(gate) * attended).astype(bf16)
    mid = (atoms + dot(gated, wo_ref[...])).astype(bf16)
    mid_ref[...] = mid
    for target in range(targets):
        hold_ref[target] = mid
    step = targets // COPIES
    late = [
        pltpu.make_async_copy(
            hold_ref.at[pl.ds(part * step, step)],
            send_ref.at[pl.ds(part * step, step), pl.ds(FIRST_ROWS, count), :],
            hold_sem.at[part],
        )
        for part in range(COPIES)
    ]
    for copy in late:
        copy.start()
    for copy in early + late:
        copy.wait()


def pair_body(pair_refs, win_ref, wout_ref, wb_ref, hold_ref):
    part, width, _ = pair_refs[0].shape
    rows = part * len(pair_refs)
    tile = jnp.concatenate([ref[...].reshape(part * width, CZ) for ref in pair_refs], axis=0)
    centred = dot_t(centre(), tile)
    spread = jnp.sum(centred * centred, axis=0, keepdims=True) * (1.0 / CZ)
    normed = (centred * lax.rsqrt(spread + epsilon)).astype(bf16)
    both = dot(win_ref[...], normed)
    half = both.shape[0] // 2
    gate, up = both[:half], both[half:]
    hidden = ((gate * jnp.tanh(gate) + gate) * up).astype(bf16)
    renewed = centred + dot(wout_ref[...], hidden)
    spread = jnp.sum(renewed * renewed, axis=0, keepdims=True) * (1.0 / CZ)
    bias = dot(wb_ref[...], renewed.astype(bf16)) * lax.rsqrt(spread + epsilon)
    for i in range(rows):
        hold_ref[:, i, :] = bias[:, i * width : (i + 1) * width]
    return hold_ref[...].astype(bf16)


def centre():
    row = lax.broadcasted_iota(jnp.int32, (CZ, CZ), 0)
    column = lax.broadcasted_iota(jnp.int32, (CZ, CZ), 1)
    return (jnp.where(row == column, 1.0, 0.0) - 1.0 / CZ).astype(bf16)


def pair_first(*refs):
    *pair_refs, trans_in_ref, trans_out_ref, wb_ref, out_ref, win_ref, wout_ref, hold_ref = refs

    @pl.when(pl.program_id(0) == 0)
    def _():
        units = win_ref.shape[0] // 2
        parts = units // CZ
        groups = regrouped(trans_in_ref[...], 2 * parts)
        for part in range(parts):
            gate, up = groups[2 * part : 2 * part + 2]
            win_ref[part * CZ : (part + 1) * CZ, :] = (gate.T * 0.5).astype(bf16)
            win_ref[units + part * CZ : units + (part + 1) * CZ, :] = up.T.astype(bf16)
        wout_ref[...] = dot_t(centre(), trans_out_ref[...]).astype(bf16)

    rows = pl.ds(pl.multiple_of(pl.program_id(0) * PAIR_ROWS, PAIR_ROWS), PAIR_ROWS)
    out_ref[:, rows, :] = pair_body(pair_refs, win_ref, wout_ref, wb_ref, hold_ref)


def pair_rest(_, early_ref, *refs):
    *pair_refs, win_ref, wout_ref, wb_ref, out_ref, done_ref, hold_ref = refs
    done_ref[...] = jnp.zeros_like(done_ref)

    @pl.when(pl.program_id(0) == 0)
    def _():
        out_ref[...] = early_ref[:, FIRST_ROWS:, :]

    @pl.when(pl.program_id(0) > 0)
    def _():
        out_ref[...] = pair_body(pair_refs, win_ref, wout_ref, wb_ref, hold_ref)


def pair_call(kernel, pair, before, weights, steps, block, out_specs, out_shape):
    cols = pair.shape[1]
    vmem = pl.BlockSpec(memory_space=pltpu.VMEM)
    positions = steps * PAIR_ROWS * cols
    return pl.pallas_call(
        kernel,
        grid=(steps,),
        in_specs=[vmem] * len(before)
        + [pl.BlockSpec((PAIR_ROWS, cols, CZ), lambda i: (block(i), 0, 0))]
        + [vmem] * len(weights),
        out_specs=out_specs,
        out_shape=out_shape,
        scratch_shapes=[pltpu.VMEM((HEADS, PAIR_ROWS, cols), f32)],
        compiler_params=params(48),
        cost_estimate=cost(positions * 620_000, positions * 288),
        name="pair_bias",
    )(*before, in_hbm(pair), *weights)


def token_kernel(
    _, got_ref, single_ref, agg_ref, w_ref, in_ref, held_ref, send_ref
):
    sources, count = got_ref.shape[0], got_ref.shape[2]
    tokens = single_ref.shape[0]
    first, ids = FIRST_ROWS, FIRST_ROWS + count
    mids = jnp.concatenate([got_ref[s, first:ids, :] for s in range(sources)], axis=0)
    features = jnp.maximum(dot(mids, agg_ref[...]), 0.0).astype(bf16)
    token = lax.broadcasted_iota(jnp.int32, (tokens, count), 0).astype(f32)
    onehot = jnp.concatenate(
        [
            jnp.where(token == got_ref[s, ids + HEAD + HEAD // 2 - 8 :, :].astype(f32)[8:9], 1.0, 0.0)
            for s in range(sources)
        ],
        axis=1,
    )
    token_count = jnp.sum(onehot, axis=1, keepdims=True)
    token_sum = dot(onehot.astype(bf16), features)
    token_in = (single_ref[...].astype(f32) + token_sum / token_count).astype(bf16)
    in_ref[...] = token_in
    norm = layer_norm(token_in.astype(f32)).astype(bf16)
    turned = dot_t(w_ref[...], norm).astype(bf16)
    held_ref[:, :tokens] = turned[:HEAD]
    held_ref[:, tokens:] = turned[3 * HEAD :]
    send_ref[...] = turned[HEAD : 3 * HEAD]


def partner(row, hop, cross):
    return (row // CORES ^ hop) * CORES + (row % CORES ^ cross)


def chip_kernel(own_ref, other_ref, out_ref):
    rows = own_ref.shape[0]
    out_ref[:rows, :] = own_ref[...]
    out_ref[rows:, :] = other_ref[...]


def attention_kernel(place_ref, held_ref, mixed_ref, got_ref, bias_ref, *refs):
    *kv_refs, send_ref = refs
    rows = len(kv_refs) * CORES
    tokens = kv_refs[0].shape[1]
    query = held_ref[:, :tokens].astype(f32).T.astype(bf16)
    per = bias_ref.shape[0] // rows
    scores, values = [], []
    for hop, kv_ref in enumerate(kv_refs):
        for cross in range(CORES):
            source = partner(place_ref[4], hop, cross) * per
            bias = jnp.concatenate(
                [
                    jnp.concatenate([got_ref[source + k, :FIRST_ROWS, :], bias_ref[source + k]], axis=0)
                    for k in range(per)
                ],
                axis=1,
            ).astype(f32)
            start = cross * 2 * HEAD
            scores.append(dot(query, kv_ref[start : start + HEAD, :]) / math.sqrt(HEAD) + bias)
            values.append(kv_ref[start + HEAD : start + 2 * HEAD, :])
    scores = jnp.concatenate(scores, axis=1)
    raised = jnp.exp(scores - jnp.max(scores, axis=-1, keepdims=True)).astype(bf16)
    values = jnp.concatenate(values, axis=1)
    ones = jnp.ones((16, values.shape[1]), bf16)
    mixed = dot_t(jnp.concatenate([values, ones], axis=0), raised)
    attended = mixed[:HEAD] / mixed[HEAD : HEAD + 1]
    gate = held_ref[:, tokens:].astype(f32)
    gated = (jax.nn.sigmoid(gate) * attended).astype(bf16)
    back = mixed_ref[...]
    for target in range(send_ref.shape[0]):
        send_ref[target, :, :tokens] = gated
        send_ref[target, :, tokens:] = back


def ready_kernel(
    place_ref, got_ref, in_ref, token_ref, mine_ref, out_w_ref, own_ref, back_ref, onehot_ref, mixed_ref
):
    sources, count = got_ref.shape[0], got_ref.shape[2]
    tokens, width = in_ref.shape
    mine = width // sources
    token_in = in_ref[...]
    start = FIRST_ROWS + count
    back_w = jnp.concatenate([got_ref[s, start : start + mine, :] for s in range(sources)], axis=0)
    half = mine // 2
    packed = [got_ref[s, start + mine :, :].astype(f32)[:half] for s in range(sources)]
    out_w = jnp.concatenate(
        [jnp.concatenate([part, pltpu.roll(part, CA // 2, 1)], axis=0) for part in packed], axis=0
    )
    mixed_ref[...] = dot(mine_ref[...], back_w).astype(bf16)
    out_w_ref[...] = out_w.T[:mine].astype(bf16)
    back_ref[...] = dot_t(back_w.astype(f32).T.astype(bf16), token_in)
    wanted = lax.broadcasted_iota(jnp.int32, (mine, width), 0) + place_ref[3] * mine
    column = lax.broadcasted_iota(jnp.int32, (mine, width), 1)
    own_ref[...] = dot_t(jnp.where(column == wanted, 1.0, 0.0).astype(bf16), token_in)
    token = lax.broadcasted_iota(jnp.int32, (tokens, count), 0)
    onehot = jnp.where(token == token_ref[...] - place_ref[1], 1.0, 0.0)
    onehot_ref[...] = onehot.T.astype(bf16)


def final_kernel(got_ref, out_w_ref, own_ref, back_ref, onehot_ref, mid_ref, single_ref, atoms_ref):
    heads, head, _ = got_ref.shape
    tokens = own_ref.shape[1]
    gated = got_ref[:, :, :tokens].reshape(heads * head, tokens)
    mixed = got_ref[:, :, tokens:].reshape(heads * head, CA)
    single_ref[...] = (own_ref[...] + dot(out_w_ref[...], gated)).astype(bf16)
    back = (back_ref[...] + dot(mixed.astype(f32).T.astype(bf16), gated)).astype(bf16)
    picked = dot_t(onehot_ref[...], back)
    atoms_ref[...] = (mid_ref[...].astype(f32) + picked).astype(bf16)


def shape(*sizes, dtype=bf16):
    return jax.ShapeDtypeStruct(sizes, dtype)


def single_step(kernel, name, in_specs, out_shape, flops, moved, operands):
    return pl.pallas_call(
        kernel,
        in_specs=in_specs,
        out_specs=[pl.BlockSpec(memory_space=pltpu.VMEM)] * len(out_shape),
        out_shape=out_shape,
        compiler_params=params(),
        cost_estimate=cost(flops, moved),
        name=name,
    )(*operands)


def gathered(copies, axis):
    return lax.all_to_all(copies, axis, split_axis=0, concat_axis=0, tiled=True)


def body(
    atoms,
    atom_pair,
    atom_token,
    single,
    pair,
    atom_w,
    atom_pair_w,
    atom_wo,
    agg_w,
    trans_in,
    trans_out,
    bias_w,
    token_w,
    token_wo,
    back_w,
):
    row_size, col_size = lax.axis_size("row"), lax.axis_size("col")
    count = atoms.shape[0]
    query_rows, width = single.shape
    head_rows = token_wo.shape[0]
    both = ("row", "col")
    devices = row_size * col_size
    pairs = [[(i, i + 1) for i in range(start, devices - 1, 2)] for start in range(2)]
    swaps = [lax.ppermute(atoms, both, pair + [(j, i) for i, j in pair]) for pair in pairs]

    device = lax.axis_index(both)
    place = jnp.stack(
        [
            device,
            lax.axis_index("row") * query_rows,
            jnp.asarray(count * devices, device.dtype),
            lax.axis_index("col"),
            lax.axis_index("row"),
        ]
    ).astype(jnp.int32)
    smem = pl.BlockSpec(memory_space=pltpu.SMEM)
    vmem = pl.BlockSpec(memory_space=pltpu.VMEM)
    token_row = atom_token.reshape(1, count)

    units = trans_in.shape[2]
    trans_rows = trans_in.reshape(CZ, 2, units // CZ, CZ).transpose(0, 2, 1, 3).reshape(2 * units, CZ)
    key_cols = pair.shape[1]
    early, win, wout = pair_call(
        pair_first,
        pair,
        (),
        (in_hbm(trans_rows), in_hbm(trans_out), in_hbm(bias_w.T)),
        EARLY_ROWS // PAIR_ROWS,
        lambda i: i,
        [vmem] * 3,
        [shape(HEADS, EARLY_ROWS, key_cols), shape(2 * units, CZ), shape(CZ, units)],
    )
    misc = head_rows // 2 + 8
    mid_send, mid, done = pl.pallas_call(
        atom_kernel,
        in_specs=[vmem, smem] + [vmem] * 10,
        out_specs=[pl.BlockSpec(memory_space=pltpu.HBM), vmem, vmem],
        out_shape=[
            pltpu.HBM((col_size, FIRST_ROWS + count + head_rows + misc, CA), bf16),
            shape(count, CA),
            DONE,
        ],
        scratch_shapes=[
            pltpu.VMEM((col_size, count, CA), bf16),
            pltpu.VMEM((col_size, head_rows + misc, CA), bf16),
            pltpu.SemaphoreType.DMA((2,)),
            pltpu.SemaphoreType.DMA((COPIES,)),
        ],
        compiler_params=params(),
        cost_estimate=cost(4_000_000_000, 2_000_000),
        name="atom_stage",
    )(early, place, swaps[0], atoms, swaps[1], atom_pair, atom_pair_w.T, token_row, atom_w.reshape(4 * CA, CA), atom_wo,
      token_wo, back_w)
    mids = gathered(mid_send, "col")
    late_rows = query_rows - FIRST_ROWS
    bias, done = pair_call(
        pair_rest,
        pair,
        (done, early),
        (win, wout, in_hbm(bias_w.T)),
        late_rows // PAIR_ROWS,
        lambda i: jnp.maximum(i, 1) + FIRST_ROWS // PAIR_ROWS,
        [pl.BlockSpec((HEADS, PAIR_ROWS, key_cols), lambda i: (0, i, 0)), vmem],
        [shape(HEADS, late_rows, key_cols), DONE],
    )
    bias_rows = gathered(bias, "col")

    turned = jnp.transpose(token_w, (1, 2, 0)).reshape(4 * HEAD, width)
    token_in, held, kv_send = single_step(
        token_kernel,
        "token_stage",
        [vmem] * 5,
        [
            shape(query_rows, width),
            shape(HEAD, 2 * query_rows),
            shape(2 * HEAD, query_rows),
        ],
        4_000_000_000,
        2_000_000,
        (done, mids, single, agg_w, turned),
    )
    across = lax.ppermute(kv_send, "row", [(i, partner(i, 0, 1)) for i in range(row_size)])
    (chip_kv,) = single_step(
        chip_kernel,
        "chip_keys",
        [vmem] * 2,
        [shape(4 * HEAD, query_rows)],
        1_000_000,
        200_000,
        (kv_send, across),
    )
    kv = [chip_kv] + [
        lax.ppermute(chip_kv, "row", [(i, partner(i, hop, 0)) for i in range(row_size)])
        for hop in range(1, row_size // CORES)
    ]
    out_w, own, back, onehot, mixed = single_step(
        ready_kernel,
        "out_ready",
        [smem] + [vmem] * 4,
        [
            shape(width // col_size, width),
            shape(width // col_size, query_rows, dtype=f32),
            shape(CA, query_rows, dtype=f32),
            shape(count, query_rows),
            shape(head_rows, CA),
        ],
        2_000_000_000,
        2_000_000,
        (place, mids, token_in, token_row, token_wo),
    )
    (gated_send,) = single_step(
        attention_kernel,
        "token_attention",
        [smem] + [vmem] * (4 + len(kv)),
        [shape(col_size, HEAD, query_rows + CA)],
        3_000_000_000,
        2_000_000,
        (place, held, mixed, mids, bias_rows, *kv),
    )
    gated = gathered(gated_send, "col")
    single_out, atoms_out = single_step(
        final_kernel,
        "token_out",
        [vmem] * 6,
        [shape(width // col_size, query_rows), shape(count, CA)],
        2_000_000_000,
        2_000_000,
        (gated, out_w, own, back, onehot, mid),
    )
    return single_out.T, atoms_out


def solution(mesh):
    in_specs = (
        P(("row", "col"), None),
        P(("row", "col"), None, None, None),
        P(("row", "col")),
        P("row", None),
        P("row", "col", None),
        P(),
        P(),
        P(),
        P(),
        P(),
        P(),
        P(),
        P(None, None, "col"),
        P("col", None),
        P("col", None),
    )
    out_specs = (P("row", "col"), P(("row", "col"), None))
    return jax.shard_map(body, mesh=mesh, in_specs=in_specs, out_specs=out_specs, check_vma=False)
```

```python
import functools
import math

import jax
import jax.numpy as jnp
from jax import lax
from jax.experimental import pallas as pl
from jax.experimental.pallas import tpu as pltpu
from jax.sharding import PartitionSpec as P

HEADS = 16
HEAD = 48
CA = 128
CZ = 128
ATOM_HEADS = 4
ATOM_HEAD = 32
QW = 32
KW = 128
RIM = (KW - QW) // 2
CORES = 2
COPIES = 4
PAIR_ROWS = 32
FIRST_ROWS = 32
EARLY_ROWS = 64
MIB = 2**20
DONE = jax.ShapeDtypeStruct((8, 128), jnp.float32)

epsilon = 1e-05
masked_score = -1e30
bf16 = jnp.bfloat16
f32 = jnp.float32


def dot(a, b):
    return jnp.dot(a, b, preferred_element_type=f32)


def dot_t(a, b):
    return lax.dot_general(a, b, (((1,), (1,)), ((), ())), preferred_element_type=f32)


def layer_norm(values):
    centred = values - jnp.mean(values, axis=-1, keepdims=True)
    spread = jnp.mean(centred * centred, axis=-1, keepdims=True)
    return centred * lax.rsqrt(spread + epsilon)


def params(mib=24):
    return pltpu.CompilerParams(vmem_limit_bytes=mib * MIB)


def in_hbm(array):
    return pltpu.with_memory_space_constraint(array, pltpu.HBM)


def cost(flops, moved):
    return pl.CostEstimate(flops=flops, bytes_accessed=moved, transcendentals=0)


def regrouped(rows, groups):
    row = lax.broadcasted_iota(jnp.int32, (CZ, CZ), 0)
    column = lax.broadcasted_iota(jnp.int32, (CZ, CZ), 1)
    length = CZ // groups
    order = jnp.where(column == (row % length) * groups + row // length, 1.0, 0.0).astype(bf16)
    blocks = [dot(order, rows[start : start + CZ]) for start in range(0, rows.shape[0], CZ)]
    return [
        jnp.concatenate([block[group * length : (group + 1) * length] for block in blocks], axis=0)
        for group in range(groups)
    ]


def atom_kernel(
    first_ref, place_ref, even_ref, own_ref, odd_ref, atom_pair_ref, pair_w_ref, token_ref, w_ref, wo_ref,
    out_w_ref, back_w_ref, send_ref, mid_ref, done_ref, hold_ref, slice_ref, block_sem, hold_sem,
):
    done_ref[...] = jnp.zeros_like(done_ref)
    device, row, last = place_ref[0], place_ref[1], place_ref[2]
    atoms = own_ref[...].astype(f32)
    count = atoms.shape[0]
    odd = device % 2 == 1
    before = jnp.where(odd, even_ref[count - RIM :, :].astype(f32), odd_ref[count - RIM :, :].astype(f32))
    after = jnp.where(odd, odd_ref[:RIM, :].astype(f32), even_ref[:RIM, :].astype(f32))
    extended = jnp.concatenate([before, atoms, after], axis=0)
    norm = layer_norm(extended).astype(bf16)
    query_all, key_all, value_all, gate_all = [
        dot(norm, part.astype(bf16)).astype(bf16) for part in regrouped(w_ref[...], 4)
    ]
    targets = send_ref.shape[0]
    rows, width = out_w_ref.shape
    mine = width // targets
    half = rows // 2
    start = FIRST_ROWS + count
    back_w = back_w_ref[...]
    out_w = out_w_ref[...].astype(f32)
    local = (token_ref[...] - row).astype(f32)
    spare = jnp.zeros((half, CA // 2 - mine), f32)
    for target in range(targets):
        part = out_w[:, target * mine : (target + 1) * mine]
        packed = jnp.concatenate([part[:half], spare, part[half:], spare], axis=1)
        slice_ref[target, :rows] = back_w
        slice_ref[target, rows:] = jnp.concatenate([packed, jnp.broadcast_to(local, (8, CA))], axis=0).astype(bf16)
    early = [
        pltpu.make_async_copy(
            first_ref.at[:, pl.ds(0, FIRST_ROWS), :], send_ref.at[:, pl.ds(0, FIRST_ROWS), :], block_sem.at[0]
        ),
        pltpu.make_async_copy(slice_ref, send_ref.at[:, pl.ds(start, rows + half + 8), :], block_sem.at[1]),
    ]
    for copy in early:
        copy.start()
    lanes = lax.broadcasted_iota(jnp.int32, (1, CA), 1) // ATOM_HEAD
    keys = lax.broadcasted_iota(jnp.int32, (1, KW), 1)
    mix = pair_w_ref[...].astype(f32)
    parts = []
    for window in range(count // QW):
        start = window * QW
        query = query_all[RIM + start : RIM + start + QW]
        query = jnp.concatenate(
            [jnp.where(lanes == head, query, jnp.zeros_like(query)) for head in range(ATOM_HEADS)], axis=0
        )
        key = key_all[start : start + KW]
        value = value_all[start : start + KW]
        planes = [atom_pair_ref[window, c].astype(f32) for c in range(atom_pair_ref.shape[1])]
        bias = []
        for head in range(ATOM_HEADS):
            total = planes[0] * mix[head : head + 1, 0:1]
            for c in range(1, len(planes)):
                total = total + planes[c] * mix[head : head + 1, c : c + 1]
            bias.append(total)
        scores = dot_t(query, key) / math.sqrt(ATOM_HEAD) + jnp.concatenate(bias, axis=0)
        position = device * count - RIM + start + keys
        scores = jnp.where((position >= 0) & (position < last), scores, masked_score)
        raised = jnp.exp(scores - jnp.max(scores, axis=-1, keepdims=True)).astype(bf16)
        mixed = dot(raised, value) / dot(raised, jnp.ones_like(value))
        out = jnp.zeros((QW, CA), f32)
        for head in range(ATOM_HEADS):
            out = out + jnp.where(lanes == head, mixed[head * QW : (head + 1) * QW], 0.0)
        parts.append(out)
    attended = jnp.concatenate(parts, axis=0)
    gate = gate_all[RIM : RIM + count].astype(f32)
    gated = (jax.nn.sigmoid(gate) * attended).astype(bf16)
    mid = (atoms + dot(gated, wo_ref[...])).astype(bf16)
    mid_ref[...] = mid
    for target in range(targets):
        hold_ref[target] = mid
    step = targets // COPIES
    late = [
        pltpu.make_async_copy(
            hold_ref.at[pl.ds(part * step, step)],
            send_ref.at[pl.ds(part * step, step), pl.ds(FIRST_ROWS, count), :],
            hold_sem.at[part],
        )
        for part in range(COPIES)
    ]
    for copy in late:
        copy.start()
    for copy in early + late:
        copy.wait()


def pair_body(pair_refs, win_ref, wout_ref, wb_ref, hold_ref):
    part, width, _ = pair_refs[0].shape
    rows = part * len(pair_refs)
    tile = jnp.concatenate([ref[...].reshape(part * width, CZ) for ref in pair_refs], axis=0)
    centred = dot_t(centre(), tile)
    spread = jnp.sum(centred * centred, axis=0, keepdims=True) * (1.0 / CZ)
    normed = (centred * lax.rsqrt(spread + epsilon)).astype(bf16)
    both = dot(win_ref[...], normed)
    half = both.shape[0] // 2
    gate, up = both[:half], both[half:]
    hidden = ((gate * jnp.tanh(gate) + gate) * up).astype(bf16)
    renewed = centred + dot(wout_ref[...], hidden)
    spread = jnp.sum(renewed * renewed, axis=0, keepdims=True) * (1.0 / CZ)
    bias = dot(wb_ref[...], renewed.astype(bf16)) * lax.rsqrt(spread + epsilon)
    for i in range(rows):
        hold_ref[:, i, :] = bias[:, i * width : (i + 1) * width]
    return hold_ref[...].astype(bf16)


def centre():
    row = lax.broadcasted_iota(jnp.int32, (CZ, CZ), 0)
    column = lax.broadcasted_iota(jnp.int32, (CZ, CZ), 1)
    return (jnp.where(row == column, 1.0, 0.0) - 1.0 / CZ).astype(bf16)


def pair_first(*refs):
    *pair_refs, trans_in_ref, trans_out_ref, wb_ref, out_ref, win_ref, wout_ref, hold_ref = refs

    @pl.when(pl.program_id(0) == 0)
    def _():
        units = win_ref.shape[0] // 2
        parts = units // CZ
        groups = regrouped(trans_in_ref[...], 2 * parts)
        for part in range(parts):
            gate, up = groups[2 * part : 2 * part + 2]
            win_ref[part * CZ : (part + 1) * CZ, :] = (gate.T * 0.5).astype(bf16)
            win_ref[units + part * CZ : units + (part + 1) * CZ, :] = up.T.astype(bf16)
        wout_ref[...] = dot_t(centre(), trans_out_ref[...]).astype(bf16)

    rows = pl.ds(pl.multiple_of(pl.program_id(0) * PAIR_ROWS, PAIR_ROWS), PAIR_ROWS)
    out_ref[:, rows, :] = pair_body(pair_refs, win_ref, wout_ref, wb_ref, hold_ref)


def pair_rest(_, early_ref, *refs):
    *pair_refs, win_ref, wout_ref, wb_ref, out_ref, done_ref, hold_ref = refs
    done_ref[...] = jnp.zeros_like(done_ref)

    @pl.when(pl.program_id(0) == 0)
    def _():
        out_ref[...] = early_ref[:, FIRST_ROWS:, :]

    @pl.when(pl.program_id(0) > 0)
    def _():
        out_ref[...] = pair_body(pair_refs, win_ref, wout_ref, wb_ref, hold_ref)


def pair_call(kernel, pair, before, weights, steps, block, out_specs, out_shape):
    cols = pair.shape[1]
    vmem = pl.BlockSpec(memory_space=pltpu.VMEM)
    positions = steps * PAIR_ROWS * cols
    return pl.pallas_call(
        kernel,
        grid=(steps,),
        in_specs=[vmem] * len(before)
        + [pl.BlockSpec((PAIR_ROWS, cols, CZ), lambda i: (block(i), 0, 0))]
        + [vmem] * len(weights),
        out_specs=out_specs,
        out_shape=out_shape,
        scratch_shapes=[pltpu.VMEM((HEADS, PAIR_ROWS, cols), f32)],
        compiler_params=params(48),
        cost_estimate=cost(positions * 620_000, positions * 288),
        name="pair_bias",
    )(*before, in_hbm(pair), *weights)


def token_kernel(
    _, got_ref, single_ref, agg_ref, w_ref, in_ref, held_ref, send_ref
):
    sources, count = got_ref.shape[0], got_ref.shape[2]
    tokens = single_ref.shape[0]
    first, ids = FIRST_ROWS, FIRST_ROWS + count
    mids = jnp.concatenate([got_ref[s, first:ids, :] for s in range(sources)], axis=0)
    features = jnp.maximum(dot(mids, agg_ref[...]), 0.0).astype(bf16)
    token = lax.broadcasted_iota(jnp.int32, (tokens, count), 0).astype(f32)
    onehot = jnp.concatenate(
        [
            jnp.where(token == got_ref[s, ids + HEAD + HEAD // 2 - 8 :, :].astype(f32)[8:9], 1.0, 0.0)
            for s in range(sources)
        ],
        axis=1,
    )
    token_count = jnp.sum(onehot, axis=1, keepdims=True)
    token_sum = dot(onehot.astype(bf16), features)
    token_in = (single_ref[...].astype(f32) + token_sum / token_count).astype(bf16)
    in_ref[...] = token_in
    norm = layer_norm(token_in.astype(f32)).astype(bf16)
    turned = dot_t(w_ref[...], norm).astype(bf16)
    held_ref[:, :tokens] = turned[:HEAD]
    held_ref[:, tokens:] = turned[3 * HEAD :]
    send_ref[...] = turned[HEAD : 3 * HEAD]


def partner(row, hop, cross):
    return (row // CORES ^ hop) * CORES + (row % CORES ^ cross)


def chip_kernel(own_ref, other_ref, out_ref):
    rows = own_ref.shape[0]
    out_ref[:rows, :] = own_ref[...]
    out_ref[rows:, :] = other_ref[...]


def attention_kernel(place_ref, held_ref, mixed_ref, got_ref, bias_ref, *refs):
    *kv_refs, send_ref = refs
    rows = len(kv_refs) * CORES
    tokens = kv_refs[0].shape[1]
    query = held_ref[:, :tokens].astype(f32).T.astype(bf16)
    per = bias_ref.shape[0] // rows
    scores, values = [], []
    for hop, kv_ref in enumerate(kv_refs):
        for cross in range(CORES):
            source = partner(place_ref[4], hop, cross) * per
            bias = jnp.concatenate(
                [
                    jnp.concatenate([got_ref[source + k, :FIRST_ROWS, :], bias_ref[source + k]], axis=0)
                    for k in range(per)
                ],
                axis=1,
            ).astype(f32)
            start = cross * 2 * HEAD
            scores.append(dot(query, kv_ref[start : start + HEAD, :]) / math.sqrt(HEAD) + bias)
            values.append(kv_ref[start + HEAD : start + 2 * HEAD, :])
    scores = jnp.concatenate(scores, axis=1)
    raised = jnp.exp(scores - jnp.max(scores, axis=-1, keepdims=True)).astype(bf16)
    values = jnp.concatenate(values, axis=1)
    ones = jnp.ones((16, values.shape[1]), bf16)
    mixed = dot_t(jnp.concatenate([values, ones], axis=0), raised)
    attended = mixed[:HEAD] / mixed[HEAD : HEAD + 1]
    gate = held_ref[:, tokens:].astype(f32)
    gated = (jax.nn.sigmoid(gate) * attended).astype(bf16)
    back = mixed_ref[...]
    for target in range(send_ref.shape[0]):
        send_ref[target, :, :tokens] = gated
        send_ref[target, :, tokens:] = back


def ready_kernel(
    place_ref, got_ref, in_ref, token_ref, mine_ref, out_w_ref, own_ref, back_ref, onehot_ref, mixed_ref
):
    sources, count = got_ref.shape[0], got_ref.shape[2]
    tokens, width = in_ref.shape
    mine = width // sources
    token_in = in_ref[...]
    start = FIRST_ROWS + count
    back_w = jnp.concatenate([got_ref[s, start : start + mine, :] for s in range(sources)], axis=0)
    half = mine // 2
    packed = [got_ref[s, start + mine :, :].astype(f32)[:half] for s in range(sources)]
    out_w = jnp.concatenate(
        [jnp.concatenate([part, pltpu.roll(part, CA // 2, 1)], axis=0) for part in packed], axis=0
    )
    mixed_ref[...] = dot(mine_ref[...], back_w).astype(bf16)
    out_w_ref[...] = out_w.T[:mine].astype(bf16)
    back_ref[...] = dot_t(back_w.astype(f32).T.astype(bf16), token_in)
    wanted = lax.broadcasted_iota(jnp.int32, (mine, width), 0) + place_ref[3] * mine
    column = lax.broadcasted_iota(jnp.int32, (mine, width), 1)
    own_ref[...] = dot_t(jnp.where(column == wanted, 1.0, 0.0).astype(bf16), token_in)
    token = lax.broadcasted_iota(jnp.int32, (tokens, count), 0)
    onehot = jnp.where(token == token_ref[...] - place_ref[1], 1.0, 0.0)
    onehot_ref[...] = onehot.T.astype(bf16)


def final_kernel(got_ref, out_w_ref, own_ref, back_ref, onehot_ref, mid_ref, single_ref, atoms_ref):
    heads, head, _ = got_ref.shape
    tokens = own_ref.shape[1]
    gated = got_ref[:, :, :tokens].reshape(heads * head, tokens)
    mixed = got_ref[:, :, tokens:].reshape(heads * head, CA)
    single_ref[...] = (own_ref[...] + dot(out_w_ref[...], gated)).astype(bf16)
    back = (back_ref[...] + dot(mixed.astype(f32).T.astype(bf16), gated)).astype(bf16)
    picked = dot_t(onehot_ref[...], back)
    atoms_ref[...] = (mid_ref[...].astype(f32) + picked).astype(bf16)


def shape(*sizes, dtype=bf16):
    return jax.ShapeDtypeStruct(sizes, dtype)


def single_step(kernel, name, in_specs, out_shape, flops, moved, operands):
    return pl.pallas_call(
        kernel,
        in_specs=in_specs,
        out_specs=[pl.BlockSpec(memory_space=pltpu.VMEM)] * len(out_shape),
        out_shape=out_shape,
        compiler_params=params(),
        cost_estimate=cost(flops, moved),
        name=name,
    )(*operands)


def gathered(copies, axis):
    return lax.all_to_all(copies, axis, split_axis=0, concat_axis=0, tiled=True)


def body(
    atoms,
    atom_pair,
    atom_token,
    single,
    pair,
    atom_w,
    atom_pair_w,
    atom_wo,
    agg_w,
    trans_in,
    trans_out,
    bias_w,
    token_w,
    token_wo,
    back_w,
):
    row_size, col_size = lax.axis_size("row"), lax.axis_size("col")
    count = atoms.shape[0]
    query_rows, width = single.shape
    head_rows = token_wo.shape[0]
    both = ("row", "col")
    devices = row_size * col_size
    pairs = [[(i, i + 1) for i in range(start, devices - 1, 2)] for start in range(2)]
    swaps = [lax.ppermute(atoms, both, pair + [(j, i) for i, j in pair]) for pair in pairs]

    device = lax.axis_index(both)
    place = jnp.stack(
        [
            device,
            lax.axis_index("row") * query_rows,
            jnp.asarray(count * devices, device.dtype),
            lax.axis_index("col"),
            lax.axis_index("row"),
        ]
    ).astype(jnp.int32)
    smem = pl.BlockSpec(memory_space=pltpu.SMEM)
    vmem = pl.BlockSpec(memory_space=pltpu.VMEM)
    token_row = atom_token.reshape(1, count)

    units = trans_in.shape[2]
    trans_rows = trans_in.reshape(CZ, 2, units // CZ, CZ).transpose(0, 2, 1, 3).reshape(2 * units, CZ)
    key_cols = pair.shape[1]
    early, win, wout = pair_call(
        pair_first,
        pair,
        (),
        (in_hbm(trans_rows), in_hbm(trans_out), in_hbm(bias_w.T)),
        EARLY_ROWS // PAIR_ROWS,
        lambda i: i,
        [vmem] * 3,
        [shape(HEADS, EARLY_ROWS, key_cols), shape(2 * units, CZ), shape(CZ, units)],
    )
    misc = head_rows // 2 + 8
    mid_send, mid, done = pl.pallas_call(
        atom_kernel,
        in_specs=[vmem, smem] + [vmem] * 10,
        out_specs=[pl.BlockSpec(memory_space=pltpu.HBM), vmem, vmem],
        out_shape=[
            pltpu.HBM((col_size, FIRST_ROWS + count + head_rows + misc, CA), bf16),
            shape(count, CA),
            DONE,
        ],
        scratch_shapes=[
            pltpu.VMEM((col_size, count, CA), bf16),
            pltpu.VMEM((col_size, head_rows + misc, CA), bf16),
            pltpu.SemaphoreType.DMA((2,)),
            pltpu.SemaphoreType.DMA((COPIES,)),
        ],
        compiler_params=params(),
        cost_estimate=cost(4_000_000_000, 2_000_000),
        name="atom_stage",
    )(early, place, swaps[0], atoms, swaps[1], atom_pair, atom_pair_w.T, token_row, atom_w.reshape(4 * CA, CA), atom_wo,
      token_wo, back_w)
    mids = gathered(mid_send, "col")
    late_rows = query_rows - FIRST_ROWS
    bias, done = pair_call(
        pair_rest,
        pair,
        (done, early),
        (win, wout, in_hbm(bias_w.T)),
        late_rows // PAIR_ROWS,
        lambda i: jnp.maximum(i, 1) + FIRST_ROWS // PAIR_ROWS,
        [pl.BlockSpec((HEADS, PAIR_ROWS, key_cols), lambda i: (0, i, 0)), vmem],
        [shape(HEADS, late_rows, key_cols), DONE],
    )
    bias_rows = gathered(bias, "col")

    turned = jnp.transpose(token_w, (1, 2, 0)).reshape(4 * HEAD, width)
    token_in, held, kv_send = single_step(
        token_kernel,
        "token_stage",
        [vmem] * 5,
        [
            shape(query_rows, width),
            shape(HEAD, 2 * query_rows),
            shape(2 * HEAD, query_rows),
        ],
        4_000_000_000,
        2_000_000,
        (done, mids, single, agg_w, turned),
    )
    across = lax.ppermute(kv_send, "row", [(i, partner(i, 0, 1)) for i in range(row_size)])
    (chip_kv,) = single_step(
        chip_kernel,
        "chip_keys",
        [vmem] * 2,
        [shape(4 * HEAD, query_rows)],
        1_000_000,
        200_000,
        (kv_send, across),
    )
    kv = [chip_kv] + [
        lax.ppermute(chip_kv, "row", [(i, partner(i, hop, 0)) for i in range(row_size)])
        for hop in range(1, row_size // CORES)
    ]
    out_w, own, back, onehot, mixed = single_step(
        ready_kernel,
        "out_ready",
        [smem] + [vmem] * 4,
        [
            shape(width // col_size, width),
            shape(width // col_size, query_rows, dtype=f32),
            shape(CA, query_rows, dtype=f32),
            shape(count, query_rows),
            shape(head_rows, CA),
        ],
        2_000_000_000,
        2_000_000,
        (place, mids, token_in, token_row, token_wo),
    )
    (gated_send,) = single_step(
        attention_kernel,
        "token_attention",
        [smem] + [vmem] * (4 + len(kv)),
        [shape(col_size, HEAD, query_rows + CA)],
        3_000_000_000,
        2_000_000,
        (place, held, mixed, mids, bias_rows, *kv),
    )
    gated = gathered(gated_send, "col")
    single_out, atoms_out = single_step(
        final_kernel,
        "token_out",
        [vmem] * 6,
        [shape(width // col_size, query_rows), shape(count, CA)],
        2_000_000_000,
        2_000_000,
        (gated, out_w, own, back, onehot, mid),
    )
    return single_out.T, atoms_out


def solution(mesh):
    in_specs = (
        P(("row", "col"), None),
        P(("row", "col"), None, None, None),
        P(("row", "col")),
        P("row", None),
        P("row", "col", None),
        P(),
        P(),
        P(),
        P(),
        P(),
        P(),
        P(),
        P(None, None, "col"),
        P("col", None),
        P("col", None),
    )
    out_specs = (P("row", "col"), P(("row", "col"), None))
    return jax.shard_map(body, mesh=mesh, in_specs=in_specs, out_specs=out_specs, check_vma=False)
```

```python
import functools
import math

import jax
import jax.numpy as jnp
from jax import lax
from jax.experimental import pallas as pl
from jax.experimental.pallas import tpu as pltpu
from jax.sharding import PartitionSpec as P

HEADS = 16
HEAD = 48
CA = 128
CZ = 128
ATOM_HEADS = 4
ATOM_HEAD = 32
QW = 32
KW = 128
RIM = (KW - QW) // 2
CORES = 2
COPIES = 4
PAIR_ROWS = 32
FIRST_ROWS = 32
EARLY_ROWS = 64
MIB = 2**20
DONE = jax.ShapeDtypeStruct((8, 128), jnp.float32)

epsilon = 1e-05
masked_score = -1e30
bf16 = jnp.bfloat16
f32 = jnp.float32


def dot(a, b):
    return jnp.dot(a, b, preferred_element_type=f32)


def dot_t(a, b):
    return lax.dot_general(a, b, (((1,), (1,)), ((), ())), preferred_element_type=f32)


def layer_norm(values):
    centred = values - jnp.mean(values, axis=-1, keepdims=True)
    spread = jnp.mean(centred * centred, axis=-1, keepdims=True)
    return centred * lax.rsqrt(spread + epsilon)


def params(mib=24):
    return pltpu.CompilerParams(vmem_limit_bytes=mib * MIB)


def in_hbm(array):
    return pltpu.with_memory_space_constraint(array, pltpu.HBM)


def cost(flops, moved):
    return pl.CostEstimate(flops=flops, bytes_accessed=moved, transcendentals=0)


def regrouped(rows, groups):
    row = lax.broadcasted_iota(jnp.int32, (CZ, CZ), 0)
    column = lax.broadcasted_iota(jnp.int32, (CZ, CZ), 1)
    length = CZ // groups
    order = jnp.where(column == (row % length) * groups + row // length, 1.0, 0.0).astype(bf16)
    blocks = [dot(order, rows[start : start + CZ]) for start in range(0, rows.shape[0], CZ)]
    return [
        jnp.concatenate([block[group * length : (group + 1) * length] for block in blocks], axis=0)
        for group in range(groups)
    ]


def atom_kernel(
    first_ref, place_ref, even_ref, own_ref, odd_ref, atom_pair_ref, pair_w_ref, token_ref, w_ref, wo_ref,
    out_w_ref, back_w_ref, send_ref, mid_ref, done_ref, hold_ref, slice_ref, block_sem, hold_sem,
):
    done_ref[...] = jnp.zeros_like(done_ref)
    device, row, last = place_ref[0], place_ref[1], place_ref[2]
    atoms = own_ref[...].astype(f32)
    count = atoms.shape[0]
    odd = device % 2 == 1
    before = jnp.where(odd, even_ref[count - RIM :, :].astype(f32), odd_ref[count - RIM :, :].astype(f32))
    after = jnp.where(odd, odd_ref[:RIM, :].astype(f32), even_ref[:RIM, :].astype(f32))
    extended = jnp.concatenate([before, atoms, after], axis=0)
    norm = layer_norm(extended).astype(bf16)
    query_all, key_all, value_all, gate_all = [
        dot(norm, part.astype(bf16)).astype(bf16) for part in regrouped(w_ref[...], 4)
    ]
    targets = send_ref.shape[0]
    rows, width = out_w_ref.shape
    mine = width // targets
    half = rows // 2
    start = FIRST_ROWS + count
    back_w = back_w_ref[...]
    out_w = out_w_ref[...].astype(f32)
    local = (token_ref[...] - row).astype(f32)
    spare = jnp.zeros((half, CA // 2 - mine), f32)
    for target in range(targets):
        part = out_w[:, target * mine : (target + 1) * mine]
        packed = jnp.concatenate([part[:half], spare, part[half:], spare], axis=1)
        slice_ref[target, :rows] = back_w
        slice_ref[target, rows:] = jnp.concatenate([packed, jnp.broadcast_to(local, (8, CA))], axis=0).astype(bf16)
    early = [
        pltpu.make_async_copy(
            first_ref.at[:, pl.ds(0, FIRST_ROWS), :], send_ref.at[:, pl.ds(0, FIRST_ROWS), :], block_sem.at[0]
        ),
        pltpu.make_async_copy(slice_ref, send_ref.at[:, pl.ds(start, rows + half + 8), :], block_sem.at[1]),
    ]
    for copy in early:
        copy.start()
    lanes = lax.broadcasted_iota(jnp.int32, (1, CA), 1) // ATOM_HEAD
    keys = lax.broadcasted_iota(jnp.int32, (1, KW), 1)
    mix = pair_w_ref[...].astype(f32)
    parts = []
    for window in range(count // QW):
        start = window * QW
        query = query_all[RIM + start : RIM + start + QW]
        query = jnp.concatenate(
            [jnp.where(lanes == head, query, jnp.zeros_like(query)) for head in range(ATOM_HEADS)], axis=0
        )
        key = key_all[start : start + KW]
        value = value_all[start : start + KW]
        planes = [atom_pair_ref[window, c].astype(f32) for c in range(atom_pair_ref.shape[1])]
        bias = []
        for head in range(ATOM_HEADS):
            total = planes[0] * mix[head : head + 1, 0:1]
            for c in range(1, len(planes)):
                total = total + planes[c] * mix[head : head + 1, c : c + 1]
            bias.append(total)
        scores = dot_t(query, key) / math.sqrt(ATOM_HEAD) + jnp.concatenate(bias, axis=0)
        position = device * count - RIM + start + keys
        scores = jnp.where((position >= 0) & (position < last), scores, masked_score)
        raised = jnp.exp(scores - jnp.max(scores, axis=-1, keepdims=True)).astype(bf16)
        mixed = dot(raised, value) / dot(raised, jnp.ones_like(value))
        out = jnp.zeros((QW, CA), f32)
        for head in range(ATOM_HEADS):
            out = out + jnp.where(lanes == head, mixed[head * QW : (head + 1) * QW], 0.0)
        parts.append(out)
    attended = jnp.concatenate(parts, axis=0)
    gate = gate_all[RIM : RIM + count].astype(f32)
    gated = (jax.nn.sigmoid(gate) * attended).astype(bf16)
    mid = (atoms + dot(gated, wo_ref[...])).astype(bf16)
    mid_ref[...] = mid
    for target in range(targets):
        hold_ref[target] = mid
    step = targets // COPIES
    late = [
        pltpu.make_async_copy(
            hold_ref.at[pl.ds(part * step, step)],
            send_ref.at[pl.ds(part * step, step), pl.ds(FIRST_ROWS, count), :],
            hold_sem.at[part],
        )
        for part in range(COPIES)
    ]
    for copy in late:
        copy.start()
    for copy in early + late:
        copy.wait()


def pair_body(pair_refs, win_ref, wout_ref, wb_ref, hold_ref):
    part, width, _ = pair_refs[0].shape
    rows = part * len(pair_refs)
    tile = jnp.concatenate([ref[...].reshape(part * width, CZ) for ref in pair_refs], axis=0)
    centred = dot_t(centre(), tile)
    spread = jnp.sum(centred * centred, axis=0, keepdims=True) * (1.0 / CZ)
    normed = (centred * lax.rsqrt(spread + epsilon)).astype(bf16)
    both = dot(win_ref[...], normed)
    half = both.shape[0] // 2
    gate, up = both[:half], both[half:]
    hidden = ((gate * jnp.tanh(gate) + gate) * up).astype(bf16)
    renewed = centred + dot(wout_ref[...], hidden)
    spread = jnp.sum(renewed * renewed, axis=0, keepdims=True) * (1.0 / CZ)
    bias = dot(wb_ref[...], renewed.astype(bf16)) * lax.rsqrt(spread + epsilon)
    for i in range(rows):
        hold_ref[:, i, :] = bias[:, i * width : (i + 1) * width]
    return hold_ref[...].astype(bf16)


def centre():
    row = lax.broadcasted_iota(jnp.int32, (CZ, CZ), 0)
    column = lax.broadcasted_iota(jnp.int32, (CZ, CZ), 1)
    return (jnp.where(row == column, 1.0, 0.0) - 1.0 / CZ).astype(bf16)


def pair_first(*refs):
    *pair_refs, trans_in_ref, trans_out_ref, wb_ref, out_ref, win_ref, wout_ref, hold_ref = refs

    @pl.when(pl.program_id(0) == 0)
    def _():
        units = win_ref.shape[0] // 2
        parts = units // CZ
        groups = regrouped(trans_in_ref[...], 2 * parts)
        for part in range(parts):
            gate, up = groups[2 * part : 2 * part + 2]
            win_ref[part * CZ : (part + 1) * CZ, :] = (gate.T * 0.5).astype(bf16)
            win_ref[units + part * CZ : units + (part + 1) * CZ, :] = up.T.astype(bf16)
        wout_ref[...] = dot_t(centre(), trans_out_ref[...]).astype(bf16)

    rows = pl.ds(pl.multiple_of(pl.program_id(0) * PAIR_ROWS, PAIR_ROWS), PAIR_ROWS)
    out_ref[:, rows, :] = pair_body(pair_refs, win_ref, wout_ref, wb_ref, hold_ref)


def pair_rest(_, early_ref, *refs):
    *pair_refs, win_ref, wout_ref, wb_ref, out_ref, done_ref, hold_ref = refs
    done_ref[...] = jnp.zeros_like(done_ref)

    @pl.when(pl.program_id(0) == 0)
    def _():
        out_ref[...] = early_ref[:, FIRST_ROWS:, :]

    @pl.when(pl.program_id(0) > 0)
    def _():
        out_ref[...] = pair_body(pair_refs, win_ref, wout_ref, wb_ref, hold_ref)


def pair_call(kernel, pair, before, weights, steps, block, out_specs, out_shape):
    cols = pair.shape[1]
    vmem = pl.BlockSpec(memory_space=pltpu.VMEM)
    positions = steps * PAIR_ROWS * cols
    return pl.pallas_call(
        kernel,
        grid=(steps,),
        in_specs=[vmem] * len(before)
        + [pl.BlockSpec((PAIR_ROWS, cols, CZ), lambda i: (block(i), 0, 0))]
        + [vmem] * len(weights),
        out_specs=out_specs,
        out_shape=out_shape,
        scratch_shapes=[pltpu.VMEM((HEADS, PAIR_ROWS, cols), f32)],
        compiler_params=params(48),
        cost_estimate=cost(positions * 620_000, positions * 288),
        name="pair_bias",
    )(*before, in_hbm(pair), *weights)


def token_kernel(
    _, got_ref, single_ref, agg_ref, w_ref, in_ref, held_ref, send_ref
):
    sources, count = got_ref.shape[0], got_ref.shape[2]
    tokens = single_ref.shape[0]
    first, ids = FIRST_ROWS, FIRST_ROWS + count
    mids = jnp.concatenate([got_ref[s, first:ids, :] for s in range(sources)], axis=0)
    features = jnp.maximum(dot(mids, agg_ref[...]), 0.0).astype(bf16)
    token = lax.broadcasted_iota(jnp.int32, (tokens, count), 0).astype(f32)
    onehot = jnp.concatenate(
        [
            jnp.where(token == got_ref[s, ids + HEAD + HEAD // 2 - 8 :, :].astype(f32)[8:9], 1.0, 0.0)
            for s in range(sources)
        ],
        axis=1,
    )
    token_count = jnp.sum(onehot, axis=1, keepdims=True)
    token_sum = dot(onehot.astype(bf16), features)
    token_in = (single_ref[...].astype(f32) + token_sum / token_count).astype(bf16)
    in_ref[...] = token_in
    norm = layer_norm(token_in.astype(f32)).astype(bf16)
    turned = dot_t(w_ref[...], norm).astype(bf16)
    held_ref[:, :tokens] = turned[:HEAD]
    held_ref[:, tokens:] = turned[3 * HEAD :]
    send_ref[...] = turned[HEAD : 3 * HEAD]


def partner(row, hop, cross):
    return (row // CORES ^ hop) * CORES + (row % CORES ^ cross)


def chip_kernel(own_ref, other_ref, out_ref):
    rows = own_ref.shape[0]
    out_ref[:rows, :] = own_ref[...]
    out_ref[rows:, :] = other_ref[...]


def attention_kernel(place_ref, held_ref, mixed_ref, got_ref, bias_ref, *refs):
    *kv_refs, send_ref = refs
    rows = len(kv_refs) * CORES
    tokens = kv_refs[0].shape[1]
    query = held_ref[:, :tokens].astype(f32).T.astype(bf16)
    per = bias_ref.shape[0] // rows
    scores, values = [], []
    for hop, kv_ref in enumerate(kv_refs):
        for cross in range(CORES):
            source = partner(place_ref[4], hop, cross) * per
            bias = jnp.concatenate(
                [
                    jnp.concatenate([got_ref[source + k, :FIRST_ROWS, :], bias_ref[source + k]], axis=0)
                    for k in range(per)
                ],
                axis=1,
            ).astype(f32)
            start = cross * 2 * HEAD
            scores.append(dot(query, kv_ref[start : start + HEAD, :]) / math.sqrt(HEAD) + bias)
            values.append(kv_ref[start + HEAD : start + 2 * HEAD, :])
    scores = jnp.concatenate(scores, axis=1)
    raised = jnp.exp(scores - jnp.max(scores, axis=-1, keepdims=True)).astype(bf16)
    values = jnp.concatenate(values, axis=1)
    ones = jnp.ones((16, values.shape[1]), bf16)
    mixed = dot_t(jnp.concatenate([values, ones], axis=0), raised)
    attended = mixed[:HEAD] / mixed[HEAD : HEAD + 1]
    gate = held_ref[:, tokens:].astype(f32)
    gated = (jax.nn.sigmoid(gate) * attended).astype(bf16)
    back = mixed_ref[...]
    for target in range(send_ref.shape[0]):
        send_ref[target, :, :tokens] = gated
        send_ref[target, :, tokens:] = back


def ready_kernel(
    place_ref, got_ref, in_ref, token_ref, mine_ref, out_w_ref, own_ref, back_ref, onehot_ref, mixed_ref
):
    sources, count = got_ref.shape[0], got_ref.shape[2]
    tokens, width = in_ref.shape
    mine = width // sources
    token_in = in_ref[...]
    start = FIRST_ROWS + count
    back_w = jnp.concatenate([got_ref[s, start : start + mine, :] for s in range(sources)], axis=0)
    half = mine // 2
    packed = [got_ref[s, start + mine :, :].astype(f32)[:half] for s in range(sources)]
    out_w = jnp.concatenate(
        [jnp.concatenate([part, pltpu.roll(part, CA // 2, 1)], axis=0) for part in packed], axis=0
    )
    mixed_ref[...] = dot(mine_ref[...], back_w).astype(bf16)
    out_w_ref[...] = out_w.T[:mine].astype(bf16)
    back_ref[...] = dot_t(back_w.astype(f32).T.astype(bf16), token_in)
    wanted = lax.broadcasted_iota(jnp.int32, (mine, width), 0) + place_ref[3] * mine
    column = lax.broadcasted_iota(jnp.int32, (mine, width), 1)
    own_ref[...] = dot_t(jnp.where(column == wanted, 1.0, 0.0).astype(bf16), token_in)
    token = lax.broadcasted_iota(jnp.int32, (tokens, count), 0)
    onehot = jnp.where(token == token_ref[...] - place_ref[1], 1.0, 0.0)
    onehot_ref[...] = onehot.T.astype(bf16)


def final_kernel(got_ref, out_w_ref, own_ref, back_ref, onehot_ref, mid_ref, single_ref, atoms_ref):
    heads, head, _ = got_ref.shape
    tokens = own_ref.shape[1]
    gated = got_ref[:, :, :tokens].reshape(heads * head, tokens)
    mixed = got_ref[:, :, tokens:].reshape(heads * head, CA)
    mine = own_ref.shape[0]
    product = dot(jnp.concatenate([out_w_ref[...], mixed.astype(f32).T.astype(bf16)], axis=0), gated)
    single_ref[...] = (own_ref[...] + product[:mine]).astype(bf16)
    back = (back_ref[...] + product[mine:]).astype(bf16)
    picked = dot_t(onehot_ref[...], back)
    atoms_ref[...] = (mid_ref[...].astype(f32) + picked).astype(bf16)


def shape(*sizes, dtype=bf16):
    return jax.ShapeDtypeStruct(sizes, dtype)


def single_step(kernel, name, in_specs, out_shape, flops, moved, operands):
    return pl.pallas_call(
        kernel,
        in_specs=in_specs,
        out_specs=[pl.BlockSpec(memory_space=pltpu.VMEM)] * len(out_shape),
        out_shape=out_shape,
        compiler_params=params(),
        cost_estimate=cost(flops, moved),
        name=name,
    )(*operands)


def gathered(copies, axis):
    return lax.all_to_all(copies, axis, split_axis=0, concat_axis=0, tiled=True)


def body(
    atoms,
    atom_pair,
    atom_token,
    single,
    pair,
    atom_w,
    atom_pair_w,
    atom_wo,
    agg_w,
    trans_in,
    trans_out,
    bias_w,
    token_w,
    token_wo,
    back_w,
):
    row_size, col_size = lax.axis_size("row"), lax.axis_size("col")
    count = atoms.shape[0]
    query_rows, width = single.shape
    head_rows = token_wo.shape[0]
    both = ("row", "col")
    devices = row_size * col_size
    pairs = [[(i, i + 1) for i in range(start, devices - 1, 2)] for start in range(2)]
    swaps = [lax.ppermute(atoms, both, pair + [(j, i) for i, j in pair]) for pair in pairs]

    device = lax.axis_index(both)
    place = jnp.stack(
        [
            device,
            lax.axis_index("row") * query_rows,
            jnp.asarray(count * devices, device.dtype),
            lax.axis_index("col"),
            lax.axis_index("row"),
        ]
    ).astype(jnp.int32)
    smem = pl.BlockSpec(memory_space=pltpu.SMEM)
    vmem = pl.BlockSpec(memory_space=pltpu.VMEM)
    token_row = atom_token.reshape(1, count)

    units = trans_in.shape[2]
    trans_rows = trans_in.reshape(CZ, 2, units // CZ, CZ).transpose(0, 2, 1, 3).reshape(2 * units, CZ)
    key_cols = pair.shape[1]
    early, win, wout = pair_call(
        pair_first,
        pair,
        (),
        (in_hbm(trans_rows), in_hbm(trans_out), in_hbm(bias_w.T)),
        EARLY_ROWS // PAIR_ROWS,
        lambda i: i,
        [vmem] * 3,
        [shape(HEADS, EARLY_ROWS, key_cols), shape(2 * units, CZ), shape(CZ, units)],
    )
    misc = head_rows // 2 + 8
    mid_send, mid, done = pl.pallas_call(
        atom_kernel,
        in_specs=[vmem, smem] + [vmem] * 10,
        out_specs=[pl.BlockSpec(memory_space=pltpu.HBM), vmem, vmem],
        out_shape=[
            pltpu.HBM((col_size, FIRST_ROWS + count + head_rows + misc, CA), bf16),
            shape(count, CA),
            DONE,
        ],
        scratch_shapes=[
            pltpu.VMEM((col_size, count, CA), bf16),
            pltpu.VMEM((col_size, head_rows + misc, CA), bf16),
            pltpu.SemaphoreType.DMA((2,)),
            pltpu.SemaphoreType.DMA((COPIES,)),
        ],
        compiler_params=params(),
        cost_estimate=cost(4_000_000_000, 2_000_000),
        name="atom_stage",
    )(early, place, swaps[0], atoms, swaps[1], atom_pair, atom_pair_w.T, token_row, atom_w.reshape(4 * CA, CA), atom_wo,
      token_wo, back_w)
    mids = gathered(mid_send, "col")
    late_rows = query_rows - FIRST_ROWS
    bias, done = pair_call(
        pair_rest,
        pair,
        (done, early),
        (win, wout, in_hbm(bias_w.T)),
        late_rows // PAIR_ROWS,
        lambda i: jnp.maximum(i, 1) + FIRST_ROWS // PAIR_ROWS,
        [pl.BlockSpec((HEADS, PAIR_ROWS, key_cols), lambda i: (0, i, 0)), vmem],
        [shape(HEADS, late_rows, key_cols), DONE],
    )
    bias_rows = gathered(bias, "col")

    turned = jnp.transpose(token_w, (1, 2, 0)).reshape(4 * HEAD, width)
    token_in, held, kv_send = single_step(
        token_kernel,
        "token_stage",
        [vmem] * 5,
        [
            shape(query_rows, width),
            shape(HEAD, 2 * query_rows),
            shape(2 * HEAD, query_rows),
        ],
        4_000_000_000,
        2_000_000,
        (done, mids, single, agg_w, turned),
    )
    across = lax.ppermute(kv_send, "row", [(i, partner(i, 0, 1)) for i in range(row_size)])
    (chip_kv,) = single_step(
        chip_kernel,
        "chip_keys",
        [vmem] * 2,
        [shape(4 * HEAD, query_rows)],
        1_000_000,
        200_000,
        (kv_send, across),
    )
    kv = [chip_kv] + [
        lax.ppermute(chip_kv, "row", [(i, partner(i, hop, 0)) for i in range(row_size)])
        for hop in range(1, row_size // CORES)
    ]
    out_w, own, back, onehot, mixed = single_step(
        ready_kernel,
        "out_ready",
        [smem] + [vmem] * 4,
        [
            shape(width // col_size, width),
            shape(width // col_size, query_rows, dtype=f32),
            shape(CA, query_rows, dtype=f32),
            shape(count, query_rows),
            shape(head_rows, CA),
        ],
        2_000_000_000,
        2_000_000,
        (place, mids, token_in, token_row, token_wo),
    )
    (gated_send,) = single_step(
        attention_kernel,
        "token_attention",
        [smem] + [vmem] * (4 + len(kv)),
        [shape(col_size, HEAD, query_rows + CA)],
        3_000_000_000,
        2_000_000,
        (place, held, mixed, mids, bias_rows, *kv),
    )
    gated = gathered(gated_send, "col")
    single_out, atoms_out = single_step(
        final_kernel,
        "token_out",
        [vmem] * 6,
        [shape(width // col_size, query_rows), shape(count, CA)],
        2_000_000_000,
        2_000_000,
        (gated, out_w, own, back, onehot, mid),
    )
    return single_out.T, atoms_out


def solution(mesh):
    in_specs = (
        P(("row", "col"), None),
        P(("row", "col"), None, None, None),
        P(("row", "col")),
        P("row", None),
        P("row", "col", None),
        P(),
        P(),
        P(),
        P(),
        P(),
        P(),
        P(),
        P(None, None, "col"),
        P("col", None),
        P("col", None),
    )
    out_specs = (P("row", "col"), P(("row", "col"), None))
    return jax.shard_map(body, mesh=mesh, in_specs=in_specs, out_specs=out_specs, check_vma=False)
```
